32 devices in a mesh: grp: 4 (over y, x), tok: 8 (over z, core).
Axes of the slice: x: 2, y: 2, z: 4, core: 2. Of those that a mesh axis runs over, the one named last changes fastest.
Arguments:
- hidden_in: bfloat16 [4, 2048, 2048], P('grp', 'tok'), may hold values from -6 to 6
- doc_ids: int32 [4, 2048], P('grp', 'tok'), may hold values from 0 to 7, never falling along the last dimension, each value on 1 to 512 neighbouring positions
- prefix_kv: bfloat16 [4, 256, 1024], P('grp', 'tok'), may hold values from -1024 to 1024
- prefix_owner: int32 [4], replicated, may hold values from 0 to 3, each once
- norm_gain: bfloat16 [2048], replicated, may hold values from 0.5 to 2
- query_gain: bfloat16 [128], replicated, may hold values from 0.59765625 to 2.390625
- key_norm_gain: bfloat16 [128], replicated, may hold values from 0.59765625 to 2.390625
- w_qkv: bfloat16 [2048, 2048], P('tok'), may hold values from -0.125 to 0.125
- w_out: bfloat16 [1024, 2048], P('tok'), may hold values from -0.1875 to 0.1875
Outputs:
- attn_out: bfloat16 [4, 2048, 2048], P('grp', 'tok')
- key_cache: bfloat16 [4, 2048, 512], P('grp', 'tok')
- value_cache: bfloat16 [4, 2048, 512], P('grp', 'tok')
The draws below stay inside these ranges and needn't reach their ends.
Inputs may be any that keep to these rules, and one draw needn't show every extreme that they name: `doc_ids`: in each group the ids never fall; every one of the 8 requests has 1 to 512 tokens, and one has exactly 512. `prefix_owner`: A permutation of the groups.
All inputs are finite; a program needn't handle non-finite values.
Results may differ from the reference program's by a relative error of at most 0.013.
The reference program's roundings to bfloat16 on the way count: a program that leaves them out, or rounds other values in their place, can miss the bound.
Values may be sent and summed in bfloat16 or wider, within the bound.
A program may use at most 128 MiB of HBM per device.

```python
import math
import jax
import jax.numpy as jnp
import numpy as np
from jax import lax

D = 2048
QUERY_HEADS = 8
KEY_VALUE_HEADS = 4
HEAD_SIZE = 128
TOK_DEV = 256
GROUPS = 4
GROUP_TOKENS = 2048
PREFIX_TOKENS = 256
MOST_SUFFIX = 512
REQ_ROW = 8
QKVW = 2048


def draw_prefix_kv(key, part):
    key_one, key_two = jax.random.split(jax.random.fold_in(key, 17), 2)
    half_width = KEY_VALUE_HEADS * HEAD_SIZE
    key_heads = jnp.clip(jax.random.normal(key_one, (GROUPS, PREFIX_TOKENS, half_width), jnp.float32), -5.0, 5.0)
    value_heads = jnp.clip(jax.random.normal(key_two, (GROUPS, PREFIX_TOKENS, half_width), jnp.float32), -5.0, 5.0)
    return jnp.concatenate([key_heads, value_heads], axis=-1).astype(jnp.bfloat16)


def shard_levels(key, shape, cuts, smallest, top_value):
    loudness, own = 1.0, jax.random.fold_in(key, 6)
    for axis_at, blocks in cuts:
        draws = jnp.exp(jax.random.uniform(jax.random.fold_in(own, axis_at), (blocks,), jnp.float32, smallest / len(cuts), top_value / len(cuts)))
        loudness = loudness * jnp.repeat(draws, shape[axis_at] // blocks).reshape([-1 if axis == axis_at else 1 for axis in range(len(shape))])
    return loudness


def split_up(number_of, total, limit, skew):
    portions = [(1 << 20) // math.isqrt(rank ** skew) + 1 for rank in range(2, number_of + 1)]
    rest, holding = total - limit - (number_of - 1), [1] * (number_of - 1)
    while rest > 0:
        free = [i for i in range(number_of - 1) if holding[i] < limit]
        pool, remaining = sum([portions[i] for i in free]), rest
        for i in free:
            addition = min(limit - holding[i], max(1, remaining * portions[i] // pool), rest)
            holding[i] = holding[i] + addition
            rest = rest - addition
    return np.array([limit] + holding)


def uneven(stream_key, number_of, total, reach, skew):
    if number_of == 2:
        one = jax.random.randint(stream_key, (), max(1, total - reach), min(reach, total - 1) + 1)
        return jnp.stack([one, total - one])
    tallies = jnp.asarray(split_up(number_of, total, reach, skew), jnp.int32)
    twos = (number_of - 1) // 2
    giver, sink = tallies[1:1 + 2 * twos:2], tallies[2:2 + 2 * twos:2]
    room = jnp.minimum(giver - 1, reach - sink)
    moved = jax.random.randint(jax.random.fold_in(stream_key, 1), (twos,), 0, 1 << 20) % (room + 1)
    tallies = tallies.at[1:1 + 2 * twos:2].set(giver - moved).at[2:2 + 2 * twos:2].set(sink + moved)
    return tallies[jax.random.permutation(jax.random.fold_in(stream_key, 2), number_of)]


def centred(rng, dims, width, limit, pieces=(), held_as=jnp.bfloat16):
    result = jax.random.normal(rng, dims, jnp.float32) * width
    if len(pieces) > 0:
        result = shard_levels(rng, dims, pieces, -0.22, 0.18) * result
    return jnp.clip(result, min=-limit, max=limit).astype(held_as)


def setup_inputs(seed: int = 0) -> dict:
    key_of = jax.random.split(jax.random.key(seed), 10)
    return {
        "hidden_in": centred(key_of[0], (GROUPS, GROUP_TOKENS, D), 1.0, 6.0, ((0, 4), (1, 8))),
        "doc_ids": jax.vmap(lambda own: jnp.searchsorted(jnp.cumsum(uneven(own, REQ_ROW, GROUP_TOKENS, MOST_SUFFIX, 2)), jnp.arange(GROUP_TOKENS), side="right"))(jax.random.split(key_of[1], GROUPS)).reshape((GROUPS, GROUP_TOKENS)).astype(jnp.int32),
        "prefix_kv": draw_prefix_kv(jax.random.fold_in(key_of[9], 71), 0),
        "prefix_owner": jax.random.permutation(key_of[3], GROUPS).astype(jnp.int32),
        "norm_gain": jnp.clip(jnp.exp(jax.random.uniform(key_of[4], (D,), jnp.float32, math.log(0.5), math.log(2.0))), 0.5, 2.0).astype(jnp.bfloat16),
        "query_gain": jnp.clip(jnp.exp(jax.random.uniform(key_of[5], (HEAD_SIZE,), jnp.float32, math.log(0.59765625), math.log(2.390625))), 0.59765625, 2.390625).astype(jnp.bfloat16),
        "key_norm_gain": jnp.clip(jnp.exp(jax.random.uniform(key_of[6], (HEAD_SIZE,), jnp.float32, math.log(0.59765625), math.log(2.390625))), 0.59765625, 2.390625).astype(jnp.bfloat16),
        "w_qkv": centred(key_of[7], (D, QKVW), D ** -0.5, 0.125, ((0, 8),)),
        "w_out": centred(key_of[8], (QUERY_HEADS * HEAD_SIZE, D), (QUERY_HEADS * HEAD_SIZE) ** -0.5, 0.1875, ((0, 8),)),
    }


epsilon = 1e-06
theta_base = 1000000.0
floor_score = -1e+30

def root_mean_scale(value_heads):
    return value_heads * lax.rsqrt(lax.optimization_barrier(jnp.mean(value_heads * value_heads, axis=-1, keepdims=True)) + epsilon)

def rotary_embed(heads, token_positions):
    half_width = heads.shape[-1] // 2
    freqs = theta_base ** (-jnp.arange(half_width, dtype=jnp.float32) / half_width)
    angles = token_positions[:, None] * freqs[None, :]
    cosine = jnp.cos(angles)[:, None, :]
    sine = jnp.sin(angles)[:, None, :]
    first = heads[..., :half_width]
    second = heads[..., half_width:]
    return jnp.concatenate([first * cosine - second * sine, second * cosine + first * sine], axis=-1)

def reference(hidden_in, doc_ids, prefix_kv, prefix_owner, norm_gain, query_gain, key_norm_gain, w_qkv, w_out):
    query_width = QUERY_HEADS * HEAD_SIZE
    key_value_width = KEY_VALUE_HEADS * HEAD_SIZE
    group_ratio = QUERY_HEADS // KEY_VALUE_HEADS
    scale = HEAD_SIZE ** (-0.5)
    outputs = []
    key_rows = []
    value_rows = []
    for group in range(GROUPS):
        tokens = hidden_in[group].astype(jnp.float32)
        normed = (root_mean_scale(tokens) * norm_gain.astype(jnp.float32)).astype(jnp.bfloat16)
        query_key_value = jnp.dot(normed, w_qkv, preferred_element_type=jnp.float32)
        ids = doc_ids[group]
        index = jnp.arange(GROUP_TOKENS, dtype=jnp.int32)
        changed = jnp.concatenate([jnp.ones((1,), dtype=jnp.bool_), ids[1:] != ids[:-1]])
        run_start = lax.cummax(jnp.where(changed, index, 0), axis=0)
        token_positions = (PREFIX_TOKENS + index - run_start).astype(jnp.float32)
        query_heads = rotary_embed(root_mean_scale(query_key_value[:, :query_width].reshape(GROUP_TOKENS, QUERY_HEADS, HEAD_SIZE)) * query_gain.astype(jnp.float32), token_positions).astype(jnp.bfloat16)
        key_heads = rotary_embed(root_mean_scale(query_key_value[:, query_width:query_width + key_value_width].reshape(GROUP_TOKENS, KEY_VALUE_HEADS, HEAD_SIZE)) * key_norm_gain.astype(jnp.float32), token_positions).astype(jnp.bfloat16)
        value_heads = query_key_value[:, query_width + key_value_width:].astype(jnp.bfloat16)
        key_flat = key_heads.reshape(GROUP_TOKENS, key_value_width)
        key_rows.append(key_flat)
        value_rows.append(value_heads)
        query_heads = lax.optimization_barrier(query_heads)
        key_heads = lax.optimization_barrier(key_heads)
        value_heads = lax.optimization_barrier(value_heads)
        owned_prefix = lax.dynamic_index_in_dim(prefix_kv, prefix_owner[group], 0, keepdims=False).astype(jnp.float32)
        cached_prefix_keys = owned_prefix[:, :key_value_width].reshape(PREFIX_TOKENS, KEY_VALUE_HEADS, HEAD_SIZE)
        cached_prefix_values = owned_prefix[:, key_value_width:].reshape(PREFIX_TOKENS, KEY_VALUE_HEADS, HEAD_SIZE)
        grouped_queries = query_heads.astype(jnp.float32).reshape(GROUP_TOKENS, KEY_VALUE_HEADS, group_ratio, HEAD_SIZE)
        padded_keys = jnp.concatenate([jnp.zeros((MOST_SUFFIX, KEY_VALUE_HEADS, HEAD_SIZE), jnp.float32), key_heads.astype(jnp.float32)], axis=0)
        padded_values = jnp.concatenate([jnp.zeros((MOST_SUFFIX, key_value_width), jnp.float32), value_heads.astype(jnp.float32)], axis=0).reshape(MOST_SUFFIX + GROUP_TOKENS, KEY_VALUE_HEADS, HEAD_SIZE)
        ids_pad = jnp.concatenate([jnp.full((MOST_SUFFIX,), -1, jnp.int32), ids])

        def block(number):
            start = number * TOK_DEV
            query_block = lax.dynamic_slice_in_dim(grouped_queries, start, TOK_DEV, 0)
            query_ids = lax.dynamic_slice_in_dim(ids, start, TOK_DEV, 0)
            near_keys = lax.dynamic_slice_in_dim(padded_keys, start, MOST_SUFFIX + TOK_DEV, 0)
            near_values = lax.dynamic_slice_in_dim(padded_values, start, MOST_SUFFIX + TOK_DEV, 0)
            near_ids = lax.dynamic_slice_in_dim(ids_pad, start, MOST_SUFFIX + TOK_DEV, 0)
            query_index = start + jnp.arange(TOK_DEV, dtype=jnp.int32)
            key_index = start - MOST_SUFFIX + jnp.arange(MOST_SUFFIX + TOK_DEV, dtype=jnp.int32)
            allowed = (query_ids[:, None] == near_ids[None, :]) & (key_index[None, :] <= query_index[:, None])
            far = jnp.einsum('rgjd,kgd->gjrk', query_block, cached_prefix_keys) * scale
            near = jnp.einsum('rgjd,kgd->gjrk', query_block, near_keys) * scale
            near = jnp.where(allowed[None, None], near, floor_score)
            top = jnp.maximum(lax.optimization_barrier(jnp.max(far, axis=-1)), lax.optimization_barrier(jnp.max(near, axis=-1)))
            far_weights = jnp.exp(far - top[..., None])
            near_weights = jnp.where(allowed[None, None], jnp.exp(near - top[..., None]), 0.0)
            total = lax.optimization_barrier(jnp.sum(far_weights, axis=-1)) + lax.optimization_barrier(jnp.sum(near_weights, axis=-1))
            far_rounded = lax.optimization_barrier(far_weights.astype(jnp.bfloat16)).astype(jnp.float32)
            near_rounded = lax.optimization_barrier(near_weights.astype(jnp.bfloat16)).astype(jnp.float32)
            mixed = jnp.einsum('gjrk,kgd->gjrd', far_rounded, cached_prefix_values) + jnp.einsum('gjrk,kgd->gjrd', near_rounded, near_values)
            attended = mixed / total[..., None]
            return jnp.transpose(attended, (2, 0, 1, 3)).reshape(TOK_DEV, query_width).astype(jnp.bfloat16)
        blocks = lax.map(block, jnp.arange(GROUP_TOKENS // TOK_DEV, dtype=jnp.int32))
        attended = blocks.reshape(GROUP_TOKENS, query_width)
        outputs.append(jnp.dot(attended, w_out, preferred_element_type=jnp.float32).astype(jnp.bfloat16))
    return (jnp.stack(outputs), jnp.stack(key_rows), jnp.stack(value_rows))
```

```python
import functools
import math

import jax
import jax.numpy as jnp
import numpy as np
from jax import lax
from jax.experimental import pallas as pl
from jax.experimental.pallas import tpu as pltpu
from jax.sharding import PartitionSpec as P

MESH = pl.DeviceIdType.MESH
epsilon = 1e-06
theta_base = 1000000.0
floor_score = -1e30
REACH = 2
BLOCK = 256


class Gather:
    def __init__(self, own, buf, send, recv, nz, split):
        self.own, self.buf, self.send, self.recv = own, buf, send, recv
        self.nz, self.split = nz, split
        g, t = lax.axis_index("grp"), lax.axis_index("tok")
        self.g, self.t = g, t
        self.z, self.c = t // 2, t % 2
        self.gx = g + 1 - 2 * (g % 2)
        self.gy = (g + 2) % 4
        self.gd = (self.gx + 2) % 4
        width = buf.shape[2]
        if split:
            q = width // 4
            self.ranges = (
                (self.g * q, q),
                (self.gx * q, q),
                (self.gy * q, q),
                (self.gd * q, q // 2),
                (self.gd * q + q // 2, q // 2),
            )
        else:
            self.ranges = ((0, width),)

    def at(self, ref, lo, width):
        if isinstance(lo, int):
            return ref.at[:, pl.ds(lo, width)]
        return ref.at[:, pl.ds(pl.multiple_of(lo, 128), width)]

    def copy(self, zz, core, lo, width, s, r, dev, own=False):
        place = self.at(self.buf.at[zz * 2 + core], lo, width)
        src = self.at(self.own, lo, width) if own else place
        return pltpu.make_async_remote_copy(
            src_ref=src,
            dst_ref=place,
            send_sem=self.send.at[s, zz],
            recv_sem=self.recv.at[r, zz],
            device_id=dev,
            device_id_type=MESH,
        )

    def dev_z(self, zz):
        return (self.g, zz * 2 + self.c)

    @property
    def sibling(self):
        return (self.g, self.z * 2 + 1 - self.c)

    def up(self, zz, own=False):
        return self.copy(zz, self.c, *self.ranges[0], 0, 0, self.dev_z(self.z + 1), own)

    def down(self, zz, own=False):
        return self.copy(zz, self.c, *self.ranges[0], 1 if own else 0, 0, self.dev_z(self.z - 1), own)

    def to_x(self, zz):
        return self.copy(zz, self.c, *self.ranges[0], 1, 1, (self.gx, self.t))

    def to_y(self, zz):
        return self.copy(zz, self.c, *self.ranges[0], 2, 2, (self.gy, self.t))

    def on_y(self, zz):
        lo, width = self.ranges[1]
        return self.copy(zz, self.c, lo, width // 2, 3, 3, (self.gy, self.t))

    def on_x(self, zz):
        lo, width = self.ranges[2]
        return self.copy(zz, self.c, lo + width // 2, width // 2, 4, 4, (self.gx, self.t))

    def across(self, zz, kind):
        return self.copy(zz, self.c, *self.ranges[kind], 5 + kind, 5 + kind, self.sibling)

    def across_own(self):
        return self.copy(self.z, self.c, 0, self.buf.shape[2], 5, 5, self.sibling, True)

    def wait_recv(self, zz, kind):
        self.copy(zz, self.c, *self.ranges[kind], kind, kind, self.sibling).wait_recv()

    def start(self):
        @pl.when(self.z + 1 < self.nz)
        def _():
            self.up(self.z, True).start()

        @pl.when(self.z > 0)
        def _():
            self.down(self.z, True).start()

        self.across_own().start()

    def arrive(self, zz):
        self.wait_recv(zz, 0)

        @pl.when((zz < self.z) & (self.z + 1 < self.nz))
        def _():
            self.up(zz).start()

        @pl.when((zz > self.z) & (self.z > 0))
        def _():
            self.down(zz).start()

        if self.split:
            self.to_x(zz).start()
            self.to_y(zz).start()
        self.across(zz, 0).start()

    def plane(self, zz):
        self.wait_recv(zz, 1)
        self.on_y(zz).start()
        self.across(zz, 1).start()
        self.wait_recv(zz, 2)
        self.on_x(zz).start()
        self.across(zz, 2).start()

    def diagonal(self, zz):
        for kind in (3, 4):
            self.wait_recv(zz, kind)
            self.across(zz, kind).start()

    def both(self, s, what):
        @pl.when((s >= 1) & (self.z - s >= 0))
        def _():
            what(self.z - s)

        @pl.when((s >= 1) & (self.z + s < self.nz))
        def _():
            what(self.z + s)

    def steps(self, first, last):
        def step(s, carry):
            self.both(s, self.arrive)
            if self.split:
                self.both(s - 1, self.plane)
                self.both(s - 2, self.diagonal)
            return carry

        lax.fori_loop(first, last, step, 0)

    def finish(self):
        def settle(zz, carry):
            @pl.when(zz != self.z)
            def _():
                for kind in range(len(self.ranges)):
                    lo, width = self.ranges[kind]
                    self.copy(
                        zz, 1 - self.c, lo, width, 5 + kind, 5 + kind, self.sibling
                    ).wait_recv()

            @pl.when(zz == self.z)
            def _():
                self.copy(
                    zz, 1 - self.c, 0, self.buf.shape[2], 5, 5, self.sibling
                ).wait_recv()

            return carry

        lax.fori_loop(0, self.nz, settle, 0)

    def sent(self):
        def settle(zz, carry):
            @pl.when(zz != self.z)
            def _():
                @pl.when((zz < self.z) & (self.z + 1 < self.nz))
                def _():
                    self.up(zz).wait_send()

                @pl.when((zz > self.z) & (self.z > 0))
                def _():
                    self.down(zz).wait_send()

                if self.split:
                    self.to_x(zz).wait_send()
                    self.to_y(zz).wait_send()
                    self.on_y(zz).wait_send()
                    self.on_x(zz).wait_send()
                for kind in range(len(self.ranges)):
                    self.across(zz, kind).wait_send()

            return carry

        lax.fori_loop(0, self.nz, settle, 0)

        @pl.when(self.z + 1 < self.nz)
        def _():
            self.up(self.z, True).wait_send()

        @pl.when(self.z > 0)
        def _():
            self.down(self.z, True).wait_send()

        self.across_own().wait_send()


def kernel(
    nt, ng,
    owner_ref, freq_ref, hidden_ref, ids_ref, prefix_ref, ngain_ref, qgain_ref, kgain_ref,
    wq_ref, wo_ref,
    out_ref, key_ref, value_ref,
    wq, wo, pall, psel, kv, ids_buf, normed, queries, attended, bias,
    q_send, q_recv, o_send, o_recv, p_send, p_recv, pa_send, pa_recv,
    id_send, id_recv, kv_send, kv_recv,
):
    g, t = lax.axis_index("grp"), lax.axis_index("tok")
    nz = nt // 2
    z, c = t // 2, t % 2
    rows = hidden_ref.shape[1]
    head = qgain_ref.shape[1]
    kvw = key_ref.shape[2]
    kv_heads = kvw // head
    qkvw = wq.shape[2]
    qw = qkvw - 2 * kvw
    ratio = (qw // head) // kv_heads
    depth = wq.shape[0] * wq.shape[1]

    barrier = pltpu.get_barrier_semaphore()

    def greet_tok(k, carry):
        pl.semaphore_signal(
            barrier, inc=1, device_id=(g, (t + k) % nt), device_id_type=MESH
        )
        return carry

    lax.fori_loop(1, nt, greet_tok, 0)
    for k in range(1, ng):
        pl.semaphore_signal(
            barrier, inc=1, device_id=((g + k) % ng, t), device_id_type=MESH
        )
    ids = ids_ref[...]
    ids_buf[0] = jnp.broadcast_to(ids, ids_buf.shape[1:])
    for back in range(1, REACH + 1):
        @pl.when(t < back)
        def _():
            ids_buf[back] = jnp.full(ids_buf.shape[1:], -1, jnp.int32)
            kv[back] = jnp.zeros(kv.shape[1:], kv.dtype)
    pl.semaphore_wait(barrier, nt - 1 + ng - 1)

    qg = Gather(wq_ref, wq, q_send, q_recv, nz, True)
    og = Gather(wo_ref, wo, o_send, o_recv, nz, True)
    pg = Gather(psel.at[t], psel, p_send, p_recv, nz, False)

    def id_copy(back):
        return pltpu.make_async_remote_copy(
            src_ref=ids_buf.at[0], dst_ref=ids_buf.at[back],
            send_sem=id_send.at[back], recv_sem=id_recv.at[back],
            device_id=(g, (t + back) % nt), device_id_type=MESH,
        )

    for back in range(1, REACH + 1):
        @pl.when(t + back < nt)
        def _():
            id_copy(back).start()

    def prefix_copy(k):
        return pltpu.make_async_remote_copy(
            src_ref=prefix_ref.at[0], dst_ref=pall.at[g],
            send_sem=pa_send.at[k], recv_sem=pa_recv.at[k],
            device_id=((g + k) % ng, t), device_id_type=MESH,
        )

    def prefix_got(k):
        return pltpu.make_async_remote_copy(
            src_ref=prefix_ref.at[0], dst_ref=pall.at[(g + ng - k) % ng],
            send_sem=pa_send.at[k], recv_sem=pa_recv.at[k],
            device_id=((g + k) % ng, t), device_id_type=MESH,
        )

    for k in range(1, ng):
        prefix_copy(k).start()
    qg.start()

    wq[t] = wq_ref[...]
    wo[t] = wo_ref[...]
    pall[g] = prefix_ref[0]

    def norm_rows(i, carry):
        at = pl.ds(pl.multiple_of(i * 64, 64), 64)
        x = hidden_ref[0, at, :].astype(jnp.float32)
        x = x * lax.rsqrt(jnp.mean(x * x, axis=-1, keepdims=True) + epsilon)
        normed[at, :] = (x * ngain_ref[...].astype(jnp.float32)).astype(jnp.bfloat16)
        return carry

    lax.fori_loop(0, rows // 64, norm_rows, 0)

    for k in range(1, ng):
        prefix_got(k).wait_recv()
    psel[t] = pall[owner_ref[g]]
    pg.start()

    for back in range(1, REACH + 1):
        @pl.when(t >= back)
        def _():
            id_copy(back).wait_recv()
    column = jnp.transpose(
        jnp.broadcast_to(ids.astype(jnp.float32), (128, rows)), (1, 0)
    )[:, :1]
    here = lax.broadcasted_iota(jnp.int32, (rows, rows), 0)
    there = lax.broadcasted_iota(jnp.int32, (rows, rows), 1)
    count = jnp.zeros((rows, 1), jnp.float32)
    for back in range(REACH + 1):
        allowed = column == ids_buf[back, 0:1, :].astype(jnp.float32)
        if back == 0:
            allowed = allowed & (there <= here)
        count += jnp.sum(jnp.where(allowed, 1.0, 0.0), axis=-1, keepdims=True)
        bias[back] = jnp.where(allowed, 0.0, floor_score)
    prefix_len = psel.shape[0] * psel.shape[1]
    position = count + (prefix_len - 1.0)
    angles = position * freq_ref[...]
    cosine = jnp.cos(angles)
    lane = lax.broadcasted_iota(jnp.int32, (rows, head), 1)
    sine = jnp.sin(angles)
    sine = jnp.where(lane < head // 2, -sine, sine)

    def arrived(s, carry):
        qg.both(s, qg.arrive)
        pg.both(s, pg.arrive)
        qg.both(s - 1, qg.plane)
        qg.both(s - 2, qg.diagonal)
        return carry

    lax.fori_loop(1, nz, arrived, 0)
    og.start()
    qg.steps(nz, nz + 2)
    qg.finish()

    def project(j):
        at = pl.ds(pl.multiple_of(j * BLOCK, BLOCK), BLOCK)
        w = wq[:, :, at].reshape(depth, BLOCK)
        return jnp.dot(normed[...], w, preferred_element_type=jnp.float32)

    def turned(block, gain):
        parts = []
        for i in range(BLOCK // head):
            a = block[:, i * head:(i + 1) * head]
            a = a * lax.rsqrt(jnp.mean(a * a, axis=-1, keepdims=True) + epsilon)
            a = a * gain
            a = a * cosine + pltpu.roll(a, head // 2, 1) * sine
            parts.append(a.astype(jnp.bfloat16))
        return jnp.concatenate(parts, axis=1)

    def key_block(j, carry):
        at = pl.ds(pl.multiple_of(j * BLOCK, BLOCK), BLOCK)
        made = turned(project(qw // BLOCK + j), kgain_ref[...].astype(jnp.float32))
        kv[0, :, at] = made
        key_ref[0, :, at] = made
        return carry

    def value_block(j, carry):
        made = project((qw + kvw) // BLOCK + j).astype(jnp.bfloat16)
        kv[0, :, pl.ds(pl.multiple_of(kvw + j * BLOCK, BLOCK), BLOCK)] = made
        value_ref[0, :, pl.ds(pl.multiple_of(j * BLOCK, BLOCK), BLOCK)] = made
        return carry

    def query_block(j, carry):
        at = pl.ds(pl.multiple_of(j * BLOCK, BLOCK), BLOCK)
        queries[:, at] = turned(project(j), qgain_ref[...].astype(jnp.float32))
        return carry

    lax.fori_loop(0, kvw // BLOCK, key_block, 0)
    lax.fori_loop(0, kvw // BLOCK, value_block, 0)

    def kv_copy(src, dst, dev):
        return pltpu.make_async_remote_copy(
            src_ref=kv.at[src], dst_ref=kv.at[dst],
            send_sem=kv_send.at[dst], recv_sem=kv_recv.at[dst],
            device_id=(g, dev), device_id_type=MESH,
        )

    to_next = kv_copy(0, 2, (t + 2) % nt)
    beside = kv_copy(0, 1, z * 2 + 1 - c)
    passed_on = kv_copy(2, 1, z * 2 + 1 - c)

    @pl.when(t + 2 < nt)
    def _():
        to_next.start()

    @pl.when(c == 0)
    def _():
        beside.start()

    lax.fori_loop(0, qw // BLOCK, query_block, 0)
    pg.finish()

    @pl.when(t >= 2)
    def _():
        to_next.wait_recv()

    @pl.when((c == 1) & (z > 0))
    def _():
        passed_on.start()

    @pl.when(t >= 1)
    def _():
        beside.wait_recv()

    factor = head ** (-0.5) * math.log2(math.e)
    dims = (((1,), (1,)), ((), ()))

    def attend(h, carry):
        kat = pl.ds(pl.multiple_of(h * head, head), head)
        vat = pl.ds(pl.multiple_of(kvw + h * head, head), head)
        q = jnp.concatenate(
            [
                queries[:, pl.ds(pl.multiple_of((h * ratio + r) * head, head), head)]
                for r in range(ratio)
            ],
            axis=0,
        )
        keys = [psel[:, :, kat].reshape(prefix_len, head)]
        values = [psel[:, :, vat].reshape(prefix_len, head)]
        for back in range(REACH + 1):
            keys.append(kv[back, :, kat])
            values.append(kv[back, :, vat])
        scores = []
        for i, k in enumerate(keys):
            s = lax.dot_general(q, k, dims, preferred_element_type=jnp.float32)
            if i:
                s = (s.reshape(ratio, rows, rows) + bias[i - 1][None]).reshape(ratio * rows, rows)
            scores.append(s)
        top = functools.reduce(
            jnp.maximum, [jnp.max(s, axis=-1, keepdims=True) for s in scores]
        )
        total, mixed = 0.0, 0.0
        for s, v in zip(scores, values):
            p = jnp.exp2((s - top) * factor)
            total += jnp.sum(p, axis=-1, keepdims=True)
            mixed += jnp.dot(p.astype(jnp.bfloat16), v, preferred_element_type=jnp.float32)
        mixed = (mixed / total).astype(jnp.bfloat16)
        for r in range(ratio):
            attended[:, pl.ds(pl.multiple_of((h * ratio + r) * head, head), head)] = mixed[
                r * rows:(r + 1) * rows
            ]
        og.steps(1 + h * per, jnp.minimum(1 + (h + 1) * per, nz + 2))
        return carry

    per = -(-(nz + 1) // kv_heads)
    lax.fori_loop(0, kv_heads, attend, 0)
    og.finish()

    def out_block(j, carry):
        at = pl.ds(pl.multiple_of(j * BLOCK, BLOCK), BLOCK)
        w = wo[:, :, at].reshape(qw, BLOCK)
        out_ref[0, :, at] = jnp.dot(
            attended[...], w, preferred_element_type=jnp.float32
        ).astype(jnp.bfloat16)
        return carry

    lax.fori_loop(0, out_ref.shape[2] // BLOCK, out_block, 0)

    for one in (qg, og, pg):
        one.sent()
    for k in range(1, ng):
        prefix_copy(k).wait_send()
    for back in range(1, REACH + 1):
        @pl.when(t + back < nt)
        def _():
            id_copy(back).wait_send()

    @pl.when(t + 2 < nt)
    def _():
        to_next.wait_send()

    @pl.when(c == 0)
    def _():
        beside.wait_send()

    @pl.when((c == 1) & (z > 0))
    def _():
        passed_on.wait_send()


def per_device(
    nt, ng,
    hidden_in, doc_ids, prefix_kv, prefix_owner, norm_gain, query_gain, key_norm_gain, w_qkv, w_out
):
    rows, width = hidden_in.shape[1:]
    head = query_gain.shape[0]
    kvw = prefix_kv.shape[2] // 2
    pre = prefix_kv.shape[1]
    qkvw = w_qkv.shape[1]
    qw = qkvw - 2 * kvw
    nz = nt // 2
    half = head // 2
    freqs = np.float32(theta_base) ** (-np.arange(half, dtype=np.float32) / np.float32(half))
    freqs = np.concatenate([freqs, freqs]).astype(np.float32)[None]
    bf = jnp.bfloat16
    vm = pl.BlockSpec(memory_space=pltpu.VMEM)
    dma = pltpu.SemaphoreType.DMA
    return pl.pallas_call(
        functools.partial(kernel, nt, ng),
        out_shape=(
            jax.ShapeDtypeStruct((1, rows, w_out.shape[1]), bf),
            jax.ShapeDtypeStruct((1, rows, kvw), bf),
            jax.ShapeDtypeStruct((1, rows, kvw), bf),
        ),
        in_specs=[pl.BlockSpec(memory_space=pltpu.SMEM)] + [vm] * 9,
        out_specs=(vm, vm, vm),
        scratch_shapes=[
            pltpu.VMEM((nt,) + w_qkv.shape, bf),
            pltpu.VMEM((nt,) + w_out.shape, bf),
            pltpu.VMEM((ng, pre, 2 * kvw), bf),
            pltpu.VMEM((nt, pre, 2 * kvw), bf),
            pltpu.VMEM((REACH + 1, rows, 2 * kvw), bf),
            pltpu.VMEM((REACH + 1, 8, rows), jnp.int32),
            pltpu.VMEM((rows, width), bf),
            pltpu.VMEM((rows, qw), bf),
            pltpu.VMEM((rows, qw), bf),
            pltpu.VMEM((REACH + 1, rows, rows), jnp.float32),
            dma((10, nz)), dma((10, nz)),
            dma((10, nz)), dma((10, nz)),
            dma((10, nz)), dma((10, nz)),
            dma((ng,)), dma((ng,)),
            dma((REACH + 1,)), dma((REACH + 1,)),
            dma((REACH + 1,)), dma((REACH + 1,)),
        ],
        compiler_params=pltpu.CompilerParams(
            collective_id=0, has_side_effects=True, vmem_limit_bytes=56 * 1024 * 1024
        ),
    )(
        prefix_owner, jnp.asarray(freqs), hidden_in, doc_ids, prefix_kv,
        norm_gain[None], query_gain[None], key_norm_gain[None], w_qkv, w_out,
    )


def solution(mesh):
    return jax.shard_map(
        functools.partial(per_device, mesh.shape["tok"], mesh.shape["grp"]),
        mesh=mesh,
        in_specs=(
            P("grp", "tok", None),
            P("grp", "tok"),
            P("grp", "tok", None),
            P(),
            P(),
            P(),
            P(),
            P("tok", None),
            P("tok", None),
        ),
        out_specs=(P("grp", "tok", None), P("grp", "tok", None), P("grp", "tok", None)),
        check_vma=False,
    )
```

```python
import functools
import math

import jax
import jax.numpy as jnp
import numpy as np
from jax import lax
from jax.experimental import pallas as pl
from jax.experimental.pallas import tpu as pltpu
from jax.sharding import PartitionSpec as P

MESH = pl.DeviceIdType.MESH
epsilon = 1e-06
theta_base = 1000000.0
floor_score = -1e30
REACH = 2
BLOCK = 256


class Gather:
    def __init__(self, own, buf, send, recv, nz, split, base=0, width=None):
        self.own, self.buf, self.send, self.recv = own, buf, send, recv
        self.nz, self.split = nz, split
        g, t = lax.axis_index("grp"), lax.axis_index("tok")
        self.g, self.t = g, t
        self.z, self.c = t // 2, t % 2
        self.gx = g + 1 - 2 * (g % 2)
        self.gy = (g + 2) % 4
        self.gd = (self.gx + 2) % 4
        width = buf.shape[2] if width is None else width
        self.whole = (base, width)
        if split:
            q = width // 4
            self.ranges = (
                (base + self.g * q, q),
                (base + self.gx * q, q),
                (base + self.gy * q, q),
                (base + self.gd * q, q // 2),
                (base + self.gd * q + q // 2, q // 2),
            )
        else:
            self.ranges = (self.whole,)

    def at(self, ref, lo, width):
        if isinstance(lo, int):
            return ref.at[:, pl.ds(lo, width)]
        return ref.at[:, pl.ds(pl.multiple_of(lo, 128), width)]

    def copy(self, zz, core, lo, width, s, r, dev, own=False):
        place = self.at(self.buf.at[zz * 2 + core], lo, width)
        src = self.at(self.own, lo, width) if own else place
        return pltpu.make_async_remote_copy(
            src_ref=src,
            dst_ref=place,
            send_sem=self.send.at[s, zz],
            recv_sem=self.recv.at[r, zz],
            device_id=dev,
            device_id_type=MESH,
        )

    def dev_z(self, zz):
        return (self.g, zz * 2 + self.c)

    @property
    def sibling(self):
        return (self.g, self.z * 2 + 1 - self.c)

    def up(self, zz, own=False):
        return self.copy(zz, self.c, *self.ranges[0], 0, 0, self.dev_z(self.z + 1), own)

    def down(self, zz, own=False):
        return self.copy(zz, self.c, *self.ranges[0], 1 if own else 0, 0, self.dev_z(self.z - 1), own)

    def to_x(self, zz):
        return self.copy(zz, self.c, *self.ranges[0], 1, 1, (self.gx, self.t))

    def to_y(self, zz):
        return self.copy(zz, self.c, *self.ranges[0], 2, 2, (self.gy, self.t))

    def on_y(self, zz):
        lo, width = self.ranges[1]
        return self.copy(zz, self.c, lo, width // 2, 3, 3, (self.gy, self.t))

    def on_x(self, zz):
        lo, width = self.ranges[2]
        return self.copy(zz, self.c, lo + width // 2, width // 2, 4, 4, (self.gx, self.t))

    def across(self, zz, kind):
        return self.copy(zz, self.c, *self.ranges[kind], 5 + kind, 5 + kind, self.sibling)

    def across_own(self):
        return self.copy(self.z, self.c, *self.whole, 5, 5, self.sibling, True)

    def wait_recv(self, zz, kind):
        self.copy(zz, self.c, *self.ranges[kind], kind, kind, self.sibling).wait_recv()

    def start(self):
        @pl.when(self.z + 1 < self.nz)
        def _():
            self.up(self.z, True).start()

        @pl.when(self.z > 0)
        def _():
            self.down(self.z, True).start()

        self.across_own().start()

    def arrive(self, zz):
        self.wait_recv(zz, 0)

        @pl.when((zz < self.z) & (self.z + 1 < self.nz))
        def _():
            self.up(zz).start()

        @pl.when((zz > self.z) & (self.z > 0))
        def _():
            self.down(zz).start()

        self.across(zz, 0).start()

    def spread(self, zz):
        self.to_x(zz).start()
        self.to_y(zz).start()

    def plane(self, zz):
        self.wait_recv(zz, 1)
        self.on_y(zz).start()
        self.across(zz, 1).start()
        self.wait_recv(zz, 2)
        self.on_x(zz).start()
        self.across(zz, 2).start()

    def diagonal(self, zz):
        for kind in (3, 4):
            self.wait_recv(zz, kind)
            self.across(zz, kind).start()

    def both(self, s, what):
        @pl.when((s >= 1) & (self.z - s >= 0))
        def _():
            what(self.z - s)

        @pl.when((s >= 1) & (self.z + s < self.nz))
        def _():
            what(self.z + s)

    def step(self, s):
        self.both(s - 1, self.plane)
        self.both(s - 2, self.diagonal)

    def finish(self):
        def settle(zz, carry):
            @pl.when(zz != self.z)
            def _():
                for kind in range(len(self.ranges)):
                    lo, width = self.ranges[kind]
                    self.copy(
                        zz, 1 - self.c, lo, width, 5 + kind, 5 + kind, self.sibling
                    ).wait_recv()

            @pl.when(zz == self.z)
            def _():
                self.copy(zz, 1 - self.c, *self.whole, 5, 5, self.sibling).wait_recv()

            return carry

        lax.fori_loop(0, self.nz, settle, 0)

    def sent(self):
        def settle(zz, carry):
            @pl.when(zz != self.z)
            def _():
                @pl.when((zz < self.z) & (self.z + 1 < self.nz))
                def _():
                    self.up(zz).wait_send()

                @pl.when((zz > self.z) & (self.z > 0))
                def _():
                    self.down(zz).wait_send()

                if self.split:
                    self.to_x(zz).wait_send()
                    self.to_y(zz).wait_send()
                    self.on_y(zz).wait_send()
                    self.on_x(zz).wait_send()
                for kind in range(len(self.ranges)):
                    self.across(zz, kind).wait_send()

            return carry

        lax.fori_loop(0, self.nz, settle, 0)

        @pl.when(self.z + 1 < self.nz)
        def _():
            self.up(self.z, True).wait_send()

        @pl.when(self.z > 0)
        def _():
            self.down(self.z, True).wait_send()

        self.across_own().wait_send()


def kernel(
    nt, ng,
    owner_ref, freq_ref, hidden_ref, ids_ref, prefix_ref, ngain_ref, qgain_ref, kgain_ref,
    wq_ref, wo_ref,
    out_ref, key_ref, value_ref,
    wq, wo, pall, psel, kv, ids_buf, normed, queries, attended, bias,
    k_send, k_recv,
    q_send, q_recv, o_send, o_recv, p_send, p_recv, pa_send, pa_recv,
    id_send, id_recv, kv_send, kv_recv,
):
    g, t = lax.axis_index("grp"), lax.axis_index("tok")
    nz = nt // 2
    z, c = t // 2, t % 2
    rows = hidden_ref.shape[1]
    head = qgain_ref.shape[1]
    kvw = key_ref.shape[2]
    kv_heads = kvw // head
    qkvw = wq.shape[2]
    qw = qkvw - 2 * kvw
    ratio = (qw // head) // kv_heads
    depth = wq.shape[0] * wq.shape[1]

    barrier = pltpu.get_barrier_semaphore()

    def greet_tok(k, carry):
        pl.semaphore_signal(
            barrier, inc=1, device_id=(g, (t + k) % nt), device_id_type=MESH
        )
        return carry

    lax.fori_loop(1, nt, greet_tok, 0)
    for k in range(1, ng):
        pl.semaphore_signal(
            barrier, inc=1, device_id=((g + k) % ng, t), device_id_type=MESH
        )
    ids = ids_ref[...]
    ids_buf[0] = jnp.broadcast_to(ids, ids_buf.shape[1:])
    for back in range(1, REACH + 1):
        @pl.when(t < back)
        def _():
            ids_buf[back] = jnp.full(ids_buf.shape[1:], -1, jnp.int32)
            kv[back] = jnp.zeros(kv.shape[1:], kv.dtype)
    pl.semaphore_wait(barrier, nt - 1 + ng - 1)

    kg = Gather(wq_ref, wq, k_send, k_recv, nz, True, qw, 2 * kvw)
    qg = Gather(wq_ref, wq, q_send, q_recv, nz, True, 0, qw)
    og = Gather(wo_ref, wo, o_send, o_recv, nz, True)
    pg = Gather(psel.at[t], psel, p_send, p_recv, nz, False)

    def id_copy(back):
        return pltpu.make_async_remote_copy(
            src_ref=ids_buf.at[0], dst_ref=ids_buf.at[back],
            send_sem=id_send.at[back], recv_sem=id_recv.at[back],
            device_id=(g, (t + back) % nt), device_id_type=MESH,
        )

    for back in range(1, REACH + 1):
        @pl.when(t + back < nt)
        def _():
            id_copy(back).start()

    def prefix_copy(k):
        return pltpu.make_async_remote_copy(
            src_ref=prefix_ref.at[0], dst_ref=pall.at[g],
            send_sem=pa_send.at[k], recv_sem=pa_recv.at[k],
            device_id=((g + k) % ng, t), device_id_type=MESH,
        )

    def prefix_got(k):
        return pltpu.make_async_remote_copy(
            src_ref=prefix_ref.at[0], dst_ref=pall.at[(g + ng - k) % ng],
            send_sem=pa_send.at[k], recv_sem=pa_recv.at[k],
            device_id=((g + k) % ng, t), device_id_type=MESH,
        )

    for k in range(1, ng):
        prefix_copy(k).start()
    kg.start()

    wq[t] = wq_ref[...]
    wo[t] = wo_ref[...]
    pall[g] = prefix_ref[0]

    def norm_rows(i, carry):
        at = pl.ds(pl.multiple_of(i * 64, 64), 64)
        x = hidden_ref[0, at, :].astype(jnp.float32)
        x = x * lax.rsqrt(jnp.mean(x * x, axis=-1, keepdims=True) + epsilon)
        normed[at, :] = (x * ngain_ref[...].astype(jnp.float32)).astype(jnp.bfloat16)
        return carry

    lax.fori_loop(0, rows // 64, norm_rows, 0)

    for k in range(1, ng):
        prefix_got(k).wait_recv()
    psel[t] = pall[owner_ref[g]]

    for back in range(1, REACH + 1):
        @pl.when(t >= back)
        def _():
            id_copy(back).wait_recv()
    column = jnp.transpose(
        jnp.broadcast_to(ids.astype(jnp.float32), (128, rows)), (1, 0)
    )[:, :1]
    here = lax.broadcasted_iota(jnp.int32, (rows, rows), 0)
    there = lax.broadcasted_iota(jnp.int32, (rows, rows), 1)
    count = jnp.zeros((rows, 1), jnp.float32)
    for back in range(REACH + 1):
        allowed = column == ids_buf[back, 0:1, :].astype(jnp.float32)
        if back == 0:
            allowed = allowed & (there <= here)
        count += jnp.sum(jnp.where(allowed, 1.0, 0.0), axis=-1, keepdims=True)
        bias[back] = jnp.where(allowed, 0.0, floor_score)
    prefix_len = psel.shape[0] * psel.shape[1]
    position = count + (prefix_len - 1.0)
    angles = position * freq_ref[...]
    cosine = jnp.cos(angles)
    lane = lax.broadcasted_iota(jnp.int32, (rows, head), 1)
    sine = jnp.sin(angles)
    sine = jnp.where(lane < head // 2, -sine, sine)

    def first(s, carry):
        kg.both(s, kg.arrive)
        kg.both(s, kg.spread)
        kg.step(s)
        return carry

    lax.fori_loop(1, nz, first, 0)
    qg.start()
    pg.start()

    def second(s, carry):
        qg.both(s, qg.arrive)
        kg.step(nz - 1 + s)
        qg.both(s, qg.spread)
        return carry

    lax.fori_loop(1, nz, second, 0)
    og.start()
    kg.finish()

    def project(j):
        at = pl.ds(pl.multiple_of(j * BLOCK, BLOCK), BLOCK)
        w = wq[:, :, at].reshape(depth, BLOCK)
        return jnp.dot(normed[...], w, preferred_element_type=jnp.float32)

    def turned(block, gain):
        parts = []
        for i in range(BLOCK // head):
            a = block[:, i * head:(i + 1) * head]
            a = a * lax.rsqrt(jnp.mean(a * a, axis=-1, keepdims=True) + epsilon)
            a = a * gain
            a = a * cosine + pltpu.roll(a, head // 2, 1) * sine
            parts.append(a.astype(jnp.bfloat16))
        return jnp.concatenate(parts, axis=1)

    def key_block(j, carry):
        at = pl.ds(pl.multiple_of(j * BLOCK, BLOCK), BLOCK)
        made = turned(project(qw // BLOCK + j), kgain_ref[...].astype(jnp.float32))
        kv[0, :, at] = made
        key_ref[0, :, at] = made
        return carry

    def value_block(j, carry):
        made = project((qw + kvw) // BLOCK + j).astype(jnp.bfloat16)
        kv[0, :, pl.ds(pl.multiple_of(kvw + j * BLOCK, BLOCK), BLOCK)] = made
        value_ref[0, :, pl.ds(pl.multiple_of(j * BLOCK, BLOCK), BLOCK)] = made
        return carry

    def query_block(j, carry):
        at = pl.ds(pl.multiple_of(j * BLOCK, BLOCK), BLOCK)
        queries[:, at] = turned(project(j), qgain_ref[...].astype(jnp.float32))
        return carry

    lax.fori_loop(0, kvw // BLOCK, key_block, 0)
    lax.fori_loop(0, kvw // BLOCK, value_block, 0)

    def kv_copy(src, dst, dev):
        return pltpu.make_async_remote_copy(
            src_ref=kv.at[src], dst_ref=kv.at[dst],
            send_sem=kv_send.at[dst], recv_sem=kv_recv.at[dst],
            device_id=(g, dev), device_id_type=MESH,
        )

    to_next = kv_copy(0, 2, (t + 2) % nt)
    beside = kv_copy(0, 1, z * 2 + 1 - c)
    passed_on = kv_copy(2, 1, z * 2 + 1 - c)

    @pl.when(t + 2 < nt)
    def _():
        to_next.start()

    @pl.when(c == 0)
    def _():
        beside.start()

    def third(s, carry):
        pg.both(s, pg.arrive)
        og.both(s, og.arrive)
        qg.step(s + 1)
        og.both(s, og.spread)
        return carry

    lax.fori_loop(1, nz, third, 0)
    qg.step(nz + 1)
    qg.finish()
    lax.fori_loop(0, qw // BLOCK, query_block, 0)
    pg.finish()

    @pl.when(t >= 2)
    def _():
        to_next.wait_recv()

    @pl.when((c == 1) & (z > 0))
    def _():
        passed_on.start()

    @pl.when(t >= 1)
    def _():
        beside.wait_recv()

    factor = head ** (-0.5) * math.log2(math.e)
    dims = (((1,), (1,)), ((), ()))

    def attend(h, carry):
        kat = pl.ds(pl.multiple_of(h * head, head), head)
        vat = pl.ds(pl.multiple_of(kvw + h * head, head), head)
        q = jnp.concatenate(
            [
                queries[:, pl.ds(pl.multiple_of((h * ratio + r) * head, head), head)]
                for r in range(ratio)
            ],
            axis=0,
        )
        keys = [psel[:, :, kat].reshape(prefix_len, head)]
        values = [psel[:, :, vat].reshape(prefix_len, head)]
        for back in range(REACH + 1):
            keys.append(kv[back, :, kat])
            values.append(kv[back, :, vat])
        scores = []
        for i, k in enumerate(keys):
            s = lax.dot_general(q, k, dims, preferred_element_type=jnp.float32)
            if i:
                s = (s.reshape(ratio, rows, rows) + bias[i - 1][None]).reshape(ratio * rows, rows)
            scores.append(s)
        top = functools.reduce(
            jnp.maximum, [jnp.max(s, axis=-1, keepdims=True) for s in scores]
        )
        total, mixed = 0.0, 0.0
        for s, v in zip(scores, values):
            p = jnp.exp2((s - top) * factor)
            total += jnp.sum(p, axis=-1, keepdims=True)
            mixed += jnp.dot(p.astype(jnp.bfloat16), v, preferred_element_type=jnp.float32)
        mixed = (mixed / total).astype(jnp.bfloat16)
        for r in range(ratio):
            attended[:, pl.ds(pl.multiple_of((h * ratio + r) * head, head), head)] = mixed[
                r * rows:(r + 1) * rows
            ]

        def fourth(s, carry):
            og.step(s)
            return carry

        lax.fori_loop(2 + h * per, jnp.minimum(2 + (h + 1) * per, nz + 2), fourth, 0)
        return carry

    per = -(-nz // kv_heads)
    lax.fori_loop(0, kv_heads, attend, 0)
    og.finish()

    def out_block(j, carry):
        at = pl.ds(pl.multiple_of(j * BLOCK, BLOCK), BLOCK)
        w = wo[:, :, at].reshape(qw, BLOCK)
        out_ref[0, :, at] = jnp.dot(
            attended[...], w, preferred_element_type=jnp.float32
        ).astype(jnp.bfloat16)
        return carry

    lax.fori_loop(0, out_ref.shape[2] // BLOCK, out_block, 0)

    for one in (kg, qg, og, pg):
        one.sent()
    for k in range(1, ng):
        prefix_copy(k).wait_send()
    for back in range(1, REACH + 1):
        @pl.when(t + back < nt)
        def _():
            id_copy(back).wait_send()

    @pl.when(t + 2 < nt)
    def _():
        to_next.wait_send()

    @pl.when(c == 0)
    def _():
        beside.wait_send()

    @pl.when((c == 1) & (z > 0))
    def _():
        passed_on.wait_send()


def per_device(
    nt, ng,
    hidden_in, doc_ids, prefix_kv, prefix_owner, norm_gain, query_gain, key_norm_gain, w_qkv, w_out
):
    rows, width = hidden_in.shape[1:]
    head = query_gain.shape[0]
    kvw = prefix_kv.shape[2] // 2
    pre = prefix_kv.shape[1]
    qkvw = w_qkv.shape[1]
    qw = qkvw - 2 * kvw
    nz = nt // 2
    half = head // 2
    freqs = np.float32(theta_base) ** (-np.arange(half, dtype=np.float32) / np.float32(half))
    freqs = np.concatenate([freqs, freqs]).astype(np.float32)[None]
    bf = jnp.bfloat16
    vm = pl.BlockSpec(memory_space=pltpu.VMEM)
    dma = pltpu.SemaphoreType.DMA
    return pl.pallas_call(
        functools.partial(kernel, nt, ng),
        out_shape=(
            jax.ShapeDtypeStruct((1, rows, w_out.shape[1]), bf),
            jax.ShapeDtypeStruct((1, rows, kvw), bf),
            jax.ShapeDtypeStruct((1, rows, kvw), bf),
        ),
        in_specs=[pl.BlockSpec(memory_space=pltpu.SMEM)] + [vm] * 9,
        out_specs=(vm, vm, vm),
        scratch_shapes=[
            pltpu.VMEM((nt,) + w_qkv.shape, bf),
            pltpu.VMEM((nt,) + w_out.shape, bf),
            pltpu.VMEM((ng, pre, 2 * kvw), bf),
            pltpu.VMEM((nt, pre, 2 * kvw), bf),
            pltpu.VMEM((REACH + 1, rows, 2 * kvw), bf),
            pltpu.VMEM((REACH + 1, 8, rows), jnp.int32),
            pltpu.VMEM((rows, width), bf),
            pltpu.VMEM((rows, qw), bf),
            pltpu.VMEM((rows, qw), bf),
            pltpu.VMEM((REACH + 1, rows, rows), jnp.float32),
            dma((10, nz)), dma((10, nz)),
            dma((10, nz)), dma((10, nz)),
            dma((10, nz)), dma((10, nz)),
            dma((10, nz)), dma((10, nz)),
            dma((ng,)), dma((ng,)),
            dma((REACH + 1,)), dma((REACH + 1,)),
            dma((REACH + 1,)), dma((REACH + 1,)),
        ],
        compiler_params=pltpu.CompilerParams(
            collective_id=0, has_side_effects=True, vmem_limit_bytes=56 * 1024 * 1024
        ),
    )(
        prefix_owner, jnp.asarray(freqs), hidden_in, doc_ids, prefix_kv,
        norm_gain[None], query_gain[None], key_norm_gain[None], w_qkv, w_out,
    )


def solution(mesh):
    return jax.shard_map(
        functools.partial(per_device, mesh.shape["tok"], mesh.shape["grp"]),
        mesh=mesh,
        in_specs=(
            P("grp", "tok", None),
            P("grp", "tok"),
            P("grp", "tok", None),
            P(),
            P(),
            P(),
            P(),
            P("tok", None),
            P("tok", None),
        ),
        out_specs=(P("grp", "tok", None), P("grp", "tok", None), P("grp", "tok", None)),
        check_vma=False,
    )
```

```python
import functools
import math

import jax
import jax.numpy as jnp
import numpy as np
from jax import lax
from jax.experimental import pallas as pl
from jax.experimental.pallas import tpu as pltpu
from jax.sharding import PartitionSpec as P

MESH = pl.DeviceIdType.MESH
epsilon = 1e-06
theta_base = 1000000.0
floor_score = -1e30
REACH = 2
BLOCK = 256


class Gather:
    def __init__(self, own, buf, send, recv, nz, split, base=0, width=None):
        self.own, self.buf, self.send, self.recv = own, buf, send, recv
        self.nz, self.split = nz, split
        g, t = lax.axis_index("grp"), lax.axis_index("tok")
        self.g, self.t = g, t
        self.z, self.c = t // 2, t % 2
        self.gx = g + 1 - 2 * (g % 2)
        self.gy = (g + 2) % 4
        self.gd = (self.gx + 2) % 4
        width = buf.shape[2] if width is None else width
        rows = buf.shape[1]
        self.whole = (0, rows, base, width)
        if not split:
            self.ranges = (self.whole,)
            return
        if rows % 128 == 0:
            q = rows // 4
            parts = [(i * q, q, base, width) for i in (self.g, self.gx, self.gy, self.gd)]
        else:
            q = width // 4
            parts = [(0, rows, base + i * q, q) for i in (self.g, self.gx, self.gy, self.gd)]
        self.ranges = tuple(parts[:3]) + tuple(self.half(parts[3], i) for i in range(2))

    def half(self, part, i):
        row, rows, col, cols = part
        if self.buf.shape[1] % 128 == 0:
            return (row + i * (rows // 2), rows // 2, col, cols)
        return (row, rows, col + i * (cols // 2), cols // 2)

    def at(self, ref, row, rows, col, cols):
        row = row if isinstance(row, int) else pl.multiple_of(row, 16)
        col = col if isinstance(col, int) else pl.multiple_of(col, 128)
        return ref.at[pl.ds(row, rows), pl.ds(col, cols)]

    def copy(self, zz, core, part, s, r, dev, own=False):
        place = self.at(self.buf.at[zz * 2 + core], *part)
        src = self.at(self.own, *part) if own else place
        return pltpu.make_async_remote_copy(
            src_ref=src,
            dst_ref=place,
            send_sem=self.send.at[s, zz],
            recv_sem=self.recv.at[r, zz],
            device_id=dev,
            device_id_type=MESH,
        )

    def dev_z(self, zz):
        return (self.g, zz * 2 + self.c)

    @property
    def sibling(self):
        return (self.g, self.z * 2 + 1 - self.c)

    def up(self, zz, own=False):
        return self.copy(zz, self.c, self.ranges[0], 0, 0, self.dev_z(self.z + 1), own)

    def down(self, zz, own=False):
        return self.copy(zz, self.c, self.ranges[0], 1 if own else 0, 0, self.dev_z(self.z - 1), own)

    def to_x(self, zz):
        return self.copy(zz, self.c, self.ranges[0], 1, 1, (self.gx, self.t))

    def to_y(self, zz):
        return self.copy(zz, self.c, self.ranges[0], 2, 2, (self.gy, self.t))

    def on_y(self, zz):
        return self.copy(zz, self.c, self.half(self.ranges[1], 0), 3, 3, (self.gy, self.t))

    def on_x(self, zz):
        return self.copy(zz, self.c, self.half(self.ranges[2], 1), 4, 4, (self.gx, self.t))

    def across(self, zz, kind):
        return self.copy(zz, self.c, self.ranges[kind], 5 + kind, 5 + kind, self.sibling)

    def across_own(self):
        return self.copy(self.z, self.c, self.whole, 5, 5, self.sibling, True)

    def wait_recv(self, zz, kind):
        self.copy(zz, self.c, self.ranges[kind], kind, kind, self.sibling).wait_recv()

    def start(self):
        @pl.when(self.z + 1 < self.nz)
        def _():
            self.up(self.z, True).start()

        @pl.when(self.z > 0)
        def _():
            self.down(self.z, True).start()

        self.across_own().start()

    def arrive(self, zz):
        self.wait_recv(zz, 0)

        @pl.when((zz < self.z) & (self.z + 1 < self.nz))
        def _():
            self.up(zz).start()

        @pl.when((zz > self.z) & (self.z > 0))
        def _():
            self.down(zz).start()

        self.across(zz, 0).start()

    def spread(self, zz):
        self.to_x(zz).start()
        self.to_y(zz).start()

    def plane(self, zz):
        self.wait_recv(zz, 1)
        self.on_y(zz).start()
        self.across(zz, 1).start()
        self.wait_recv(zz, 2)
        self.on_x(zz).start()
        self.across(zz, 2).start()

    def diagonal(self, zz):
        for kind in (3, 4):
            self.wait_recv(zz, kind)
            self.across(zz, kind).start()

    def both(self, s, what):
        @pl.when((s >= 1) & (self.z - s >= 0))
        def _():
            what(self.z - s)

        @pl.when((s >= 1) & (self.z + s < self.nz))
        def _():
            what(self.z + s)

    def step(self, s):
        self.both(s - 1, self.plane)
        self.both(s - 2, self.diagonal)

    def finish(self):
        def settle(zz, carry):
            @pl.when(zz != self.z)
            def _():
                for kind in range(len(self.ranges)):
                    self.copy(
                        zz, 1 - self.c, self.ranges[kind], 5 + kind, 5 + kind, self.sibling
                    ).wait_recv()

            @pl.when(zz == self.z)
            def _():
                self.copy(zz, 1 - self.c, self.whole, 5, 5, self.sibling).wait_recv()

            return carry

        lax.fori_loop(0, self.nz, settle, 0)

    def sent(self):
        def settle(zz, carry):
            @pl.when(zz != self.z)
            def _():
                @pl.when((zz < self.z) & (self.z + 1 < self.nz))
                def _():
                    self.up(zz).wait_send()

                @pl.when((zz > self.z) & (self.z > 0))
                def _():
                    self.down(zz).wait_send()

                if self.split:
                    self.to_x(zz).wait_send()
                    self.to_y(zz).wait_send()
                    self.on_y(zz).wait_send()
                    self.on_x(zz).wait_send()
                for kind in range(len(self.ranges)):
                    self.across(zz, kind).wait_send()

            return carry

        lax.fori_loop(0, self.nz, settle, 0)

        @pl.when(self.z + 1 < self.nz)
        def _():
            self.up(self.z, True).wait_send()

        @pl.when(self.z > 0)
        def _():
            self.down(self.z, True).wait_send()

        self.across_own().wait_send()


def kernel(
    nt, ng,
    owner_ref, freq_ref, hidden_ref, ids_ref, prefix_ref, ngain_ref, qgain_ref, kgain_ref,
    wq_ref, wo_ref,
    out_ref, key_ref, value_ref,
    wq, wo, pall, psel, kv, ids_buf, normed, queries, attended, bias,
    k_send, k_recv,
    q_send, q_recv, o_send, o_recv, p_send, p_recv, pa_send, pa_recv,
    id_send, id_recv, kv_send, kv_recv,
):
    g, t = lax.axis_index("grp"), lax.axis_index("tok")
    nz = nt // 2
    z, c = t // 2, t % 2
    rows = hidden_ref.shape[1]
    head = qgain_ref.shape[1]
    kvw = key_ref.shape[2]
    kv_heads = kvw // head
    qkvw = wq.shape[2]
    qw = qkvw - 2 * kvw
    ratio = (qw // head) // kv_heads
    depth = wq.shape[0] * wq.shape[1]

    barrier = pltpu.get_barrier_semaphore()

    def greet_tok(k, carry):
        pl.semaphore_signal(
            barrier, inc=1, device_id=(g, (t + k) % nt), device_id_type=MESH
        )
        return carry

    lax.fori_loop(1, nt, greet_tok, 0)
    for k in range(1, ng):
        pl.semaphore_signal(
            barrier, inc=1, device_id=((g + k) % ng, t), device_id_type=MESH
        )
    ids = ids_ref[...]
    ids_buf[0] = jnp.broadcast_to(ids, ids_buf.shape[1:])
    for back in range(1, REACH + 1):
        @pl.when(t < back)
        def _():
            ids_buf[back] = jnp.full(ids_buf.shape[1:], -1, jnp.int32)
            kv[back] = jnp.zeros(kv.shape[1:], kv.dtype)
    pl.semaphore_wait(barrier, nt - 1 + ng - 1)

    kg = Gather(wq_ref, wq, k_send, k_recv, nz, True, qw, 2 * kvw)
    qg = Gather(wq_ref, wq, q_send, q_recv, nz, True, 0, qw)
    og = Gather(wo_ref, wo, o_send, o_recv, nz, True)
    pg = Gather(psel.at[t], psel, p_send, p_recv, nz, False)

    def id_copy(back):
        return pltpu.make_async_remote_copy(
            src_ref=ids_buf.at[0], dst_ref=ids_buf.at[back],
            send_sem=id_send.at[back], recv_sem=id_recv.at[back],
            device_id=(g, (t + back) % nt), device_id_type=MESH,
        )

    for back in range(1, REACH + 1):
        @pl.when(t + back < nt)
        def _():
            id_copy(back).start()

    def prefix_copy(k):
        return pltpu.make_async_remote_copy(
            src_ref=prefix_ref.at[0], dst_ref=pall.at[g],
            send_sem=pa_send.at[k], recv_sem=pa_recv.at[k],
            device_id=((g + k) % ng, t), device_id_type=MESH,
        )

    def prefix_got(k):
        return pltpu.make_async_remote_copy(
            src_ref=prefix_ref.at[0], dst_ref=pall.at[(g + ng - k) % ng],
            send_sem=pa_send.at[k], recv_sem=pa_recv.at[k],
            device_id=((g + k) % ng, t), device_id_type=MESH,
        )

    for k in range(1, ng):
        prefix_copy(k).start()
    kg.start()

    wq[t] = wq_ref[...]
    wo[t] = wo_ref[...]
    pall[g] = prefix_ref[0]

    def norm_rows(i, carry):
        at = pl.ds(pl.multiple_of(i * 64, 64), 64)
        x = hidden_ref[0, at, :].astype(jnp.float32)
        x = x * lax.rsqrt(jnp.mean(x * x, axis=-1, keepdims=True) + epsilon)
        normed[at, :] = (x * ngain_ref[...].astype(jnp.float32).reshape(1, -1)).astype(jnp.bfloat16)
        return carry

    lax.fori_loop(0, rows // 64, norm_rows, 0)

    for k in range(1, ng):
        prefix_got(k).wait_recv()
    psel[t] = pall[owner_ref[g]]

    for back in range(1, REACH + 1):
        @pl.when(t >= back)
        def _():
            id_copy(back).wait_recv()
    column = jnp.transpose(
        jnp.broadcast_to(ids.astype(jnp.float32), (128, rows)), (1, 0)
    )[:, :1]
    here = lax.broadcasted_iota(jnp.int32, (rows, rows), 0)
    there = lax.broadcasted_iota(jnp.int32, (rows, rows), 1)
    count = jnp.zeros((rows, 1), jnp.float32)
    for back in range(REACH + 1):
        allowed = column == ids_buf[back, 0:1, :].astype(jnp.float32)
        if back == 0:
            allowed = allowed & (there <= here)
        count += jnp.sum(jnp.where(allowed, 1.0, 0.0), axis=-1, keepdims=True)
        bias[back] = jnp.where(allowed, 0.0, floor_score)
    prefix_len = psel.shape[0] * psel.shape[1]
    position = count + (prefix_len - 1.0)
    angles = position * freq_ref[...]
    cosine = jnp.cos(angles)
    lane = lax.broadcasted_iota(jnp.int32, (rows, head), 1)
    sine = jnp.sin(angles)
    sine = jnp.where(lane < head // 2, -sine, sine)

    def first(s, carry):
        kg.both(s, kg.arrive)
        kg.both(s, kg.spread)
        kg.step(s)
        return carry

    lax.fori_loop(1, nz, first, 0)
    qg.start()
    pg.start()

    def second(s, carry):
        qg.both(s, qg.arrive)
        kg.step(nz - 1 + s)
        qg.both(s, qg.spread)
        return carry

    lax.fori_loop(1, nz, second, 0)
    kg.finish()

    def project(j):
        at = pl.ds(pl.multiple_of(j * BLOCK, BLOCK), BLOCK)
        w = wq[:, :, at].reshape(depth, BLOCK)
        return jnp.dot(normed[...], w, preferred_element_type=jnp.float32)

    def turned(block, gain):
        parts = []
        for i in range(BLOCK // head):
            a = block[:, i * head:(i + 1) * head]
            a = a * lax.rsqrt(jnp.mean(a * a, axis=-1, keepdims=True) + epsilon)
            a = a * gain
            a = a * cosine + pltpu.roll(a, head // 2, 1) * sine
            parts.append(a.astype(jnp.bfloat16))
        return jnp.concatenate(parts, axis=1)

    def key_block(j, carry):
        at = pl.ds(pl.multiple_of(j * BLOCK, BLOCK), BLOCK)
        made = turned(project(qw // BLOCK + j), kgain_ref[...].astype(jnp.float32))
        kv[0, :, at] = made
        key_ref[0, :, at] = made
        return carry

    def value_block(j, carry):
        made = project((qw + kvw) // BLOCK + j).astype(jnp.bfloat16)
        kv[0, :, pl.ds(pl.multiple_of(kvw + j * BLOCK, BLOCK), BLOCK)] = made
        value_ref[0, :, pl.ds(pl.multiple_of(j * BLOCK, BLOCK), BLOCK)] = made
        return carry

    def query_block(j, carry):
        at = pl.ds(pl.multiple_of(j * BLOCK, BLOCK), BLOCK)
        queries[:, at] = turned(project(j), qgain_ref[...].astype(jnp.float32))
        return carry

    lax.fori_loop(0, kvw // BLOCK, key_block, 0)
    lax.fori_loop(0, kvw // BLOCK, value_block, 0)

    def kv_copy(src, dst, dev):
        return pltpu.make_async_remote_copy(
            src_ref=kv.at[src], dst_ref=kv.at[dst],
            send_sem=kv_send.at[dst], recv_sem=kv_recv.at[dst],
            device_id=(g, dev), device_id_type=MESH,
        )

    to_next = kv_copy(0, 2, (t + 2) % nt)
    beside = kv_copy(0, 1, z * 2 + 1 - c)
    passed_on = kv_copy(2, 1, z * 2 + 1 - c)

    @pl.when(t + 2 < nt)
    def _():
        to_next.start()

    @pl.when(c == 0)
    def _():
        beside.start()

    og.start()

    def third(s, carry):
        pg.both(s, pg.arrive)
        qg.step(s + 1)
        return carry

    lax.fori_loop(1, nz, third, 0)
    qg.step(nz + 1)
    qg.finish()
    lax.fori_loop(0, qw // BLOCK, query_block, 0)
    pg.finish()

    def fourth(s, carry):
        og.both(s, og.arrive)
        og.both(s, og.spread)
        og.step(s)
        return carry

    fourth(1, 0)

    @pl.when(t >= 2)
    def _():
        to_next.wait_recv()

    @pl.when((c == 1) & (z > 0))
    def _():
        passed_on.start()

    @pl.when(t >= 1)
    def _():
        beside.wait_recv()

    factor = head ** (-0.5) * math.log2(math.e)
    dims = (((1,), (1,)), ((), ()))

    def attend(h, carry):
        kat = pl.ds(pl.multiple_of(h * head, head), head)
        vat = pl.ds(pl.multiple_of(kvw + h * head, head), head)
        q = jnp.concatenate(
            [
                queries[:, pl.ds(pl.multiple_of((h * ratio + r) * head, head), head)]
                for r in range(ratio)
            ],
            axis=0,
        )
        keys = [psel[:, :, kat].reshape(prefix_len, head)]
        values = [psel[:, :, vat].reshape(prefix_len, head)]
        for back in range(REACH + 1):
            keys.append(kv[back, :, kat])
            values.append(kv[back, :, vat])
        scores = []
        for i, k in enumerate(keys):
            s = lax.dot_general(q, k, dims, preferred_element_type=jnp.float32)
            if i:
                s = (s.reshape(ratio, rows, rows) + bias[i - 1][None]).reshape(ratio * rows, rows)
            scores.append(s)
        top = functools.reduce(
            jnp.maximum, [jnp.max(s, axis=-1, keepdims=True) for s in scores]
        )
        total, mixed = 0.0, 0.0
        for s, v in zip(scores, values):
            p = jnp.exp2((s - top) * factor)
            total += jnp.sum(p, axis=-1, keepdims=True)
            mixed += jnp.dot(p.astype(jnp.bfloat16), v, preferred_element_type=jnp.float32)
        mixed = (mixed / total).astype(jnp.bfloat16)
        for r in range(ratio):
            attended[:, pl.ds(pl.multiple_of((h * ratio + r) * head, head), head)] = mixed[
                r * rows:(r + 1) * rows
            ]

        lax.fori_loop(2 + h * per, jnp.minimum(2 + (h + 1) * per, nz + 2), fourth, 0)
        return carry

    per = -(-nz // kv_heads)
    lax.fori_loop(0, kv_heads, attend, 0)
    og.finish()

    def out_block(j, carry):
        at = pl.ds(pl.multiple_of(j * BLOCK, BLOCK), BLOCK)
        w = wo[:, :, at].reshape(qw, BLOCK)
        out_ref[0, :, at] = jnp.dot(
            attended[...], w, preferred_element_type=jnp.float32
        ).astype(jnp.bfloat16)
        return carry

    lax.fori_loop(0, out_ref.shape[2] // BLOCK, out_block, 0)

    for one in (kg, qg, og, pg):
        one.sent()
    for k in range(1, ng):
        prefix_copy(k).wait_send()
    for back in range(1, REACH + 1):
        @pl.when(t + back < nt)
        def _():
            id_copy(back).wait_send()

    @pl.when(t + 2 < nt)
    def _():
        to_next.wait_send()

    @pl.when(c == 0)
    def _():
        beside.wait_send()

    @pl.when((c == 1) & (z > 0))
    def _():
        passed_on.wait_send()


def place(*refs):
    count = (len(refs) - 1) // 2
    sems = refs[-1]
    copies = [
        pltpu.make_async_copy(refs[i], refs[count + i], sems.at[i]) for i in range(count)
    ]
    for one in copies:
        one.start()
    for one in copies:
        one.wait()


def per_device(
    nt, ng,
    hidden_in, doc_ids, prefix_kv, prefix_owner, norm_gain, query_gain, key_norm_gain, w_qkv, w_out
):
    rows, width = hidden_in.shape[1:]
    head = query_gain.shape[0]
    kvw = prefix_kv.shape[2] // 2
    pre = prefix_kv.shape[1]
    qkvw = w_qkv.shape[1]
    qw = qkvw - 2 * kvw
    nz = nt // 2
    half = head // 2
    freqs = np.float32(theta_base) ** (-np.arange(half, dtype=np.float32) / np.float32(half))
    freqs = np.concatenate([freqs, freqs]).astype(np.float32)[None]
    bf = jnp.bfloat16
    vm = pl.BlockSpec(memory_space=pltpu.VMEM)
    dma = pltpu.SemaphoreType.DMA
    made = pl.pallas_call(
        functools.partial(kernel, nt, ng),
        out_shape=(
            jax.ShapeDtypeStruct((1, rows, w_out.shape[1]), bf),
            jax.ShapeDtypeStruct((1, rows, kvw), bf),
            jax.ShapeDtypeStruct((1, rows, kvw), bf),
        ),
        in_specs=[pl.BlockSpec(memory_space=pltpu.SMEM)] + [vm] * 9,
        out_specs=(vm, vm, vm),
        scratch_shapes=[
            pltpu.VMEM((nt,) + w_qkv.shape, bf),
            pltpu.VMEM((nt,) + w_out.shape, bf),
            pltpu.VMEM((ng, pre, 2 * kvw), bf),
            pltpu.VMEM((nt, pre, 2 * kvw), bf),
            pltpu.VMEM((REACH + 1, rows, 2 * kvw), bf),
            pltpu.VMEM((REACH + 1, 8, rows), jnp.int32),
            pltpu.VMEM((rows, width), bf),
            pltpu.VMEM((rows, qw), bf),
            pltpu.VMEM((rows, qw), bf),
            pltpu.VMEM((REACH + 1, rows, rows), jnp.float32),
            dma((10, nz)), dma((10, nz)),
            dma((10, nz)), dma((10, nz)),
            dma((10, nz)), dma((10, nz)),
            dma((10, nz)), dma((10, nz)),
            dma((ng,)), dma((ng,)),
            dma((REACH + 1,)), dma((REACH + 1,)),
            dma((REACH + 1,)), dma((REACH + 1,)),
        ],
        compiler_params=pltpu.CompilerParams(
            collective_id=0, has_side_effects=True, vmem_limit_bytes=56 * 1024 * 1024
        ),
    )(
        prefix_owner, jnp.asarray(freqs), hidden_in, doc_ids, prefix_kv,
        norm_gain, query_gain[None], key_norm_gain[None], w_qkv, w_out,
    )
    anywhere = pl.BlockSpec(memory_space=pl.ANY)
    return pl.pallas_call(
        place,
        out_shape=tuple(jax.ShapeDtypeStruct(x.shape, x.dtype) for x in made),
        in_specs=[anywhere] * len(made),
        out_specs=(anywhere,) * len(made),
        scratch_shapes=[dma((len(made),))],
        compiler_params=pltpu.CompilerParams(vmem_limit_bytes=63 * 1024 * 1024),
    )(*made)


def solution(mesh):
    return jax.shard_map(
        functools.partial(per_device, mesh.shape["tok"], mesh.shape["grp"]),
        mesh=mesh,
        in_specs=(
            P("grp", "tok", None),
            P("grp", "tok"),
            P("grp", "tok", None),
            P(),
            P(),
            P(),
            P(),
            P("tok", None),
            P("tok", None),
        ),
        out_specs=(P("grp", "tok", None), P("grp", "tok", None), P("grp", "tok", None)),
        check_vma=False,
    )
```

```python
import functools
import math

import jax
import jax.numpy as jnp
import numpy as np
from jax import lax
from jax.experimental import pallas as pl
from jax.experimental.pallas import tpu as pltpu
from jax.sharding import PartitionSpec as P

MESH = pl.DeviceIdType.MESH
epsilon = 1e-06
theta_base = 1000000.0
floor_score = -1e30
REACH = 2
BLOCK = 256


class Gather:
    def __init__(self, own, buf, send, recv, nz, split, base=0, width=None):
        self.own, self.buf, self.send, self.recv = own, buf, send, recv
        self.nz, self.split = nz, split
        g, t = lax.axis_index("grp"), lax.axis_index("tok")
        self.g, self.t = g, t
        self.z, self.c = t // 2, t % 2
        self.gx = g + 1 - 2 * (g % 2)
        self.gy = (g + 2) % 4
        self.gd = (self.gx + 2) % 4
        width = buf.shape[2] if width is None else width
        rows = buf.shape[1]
        self.whole = (0, rows, base, width)
        if not split:
            self.ranges = (self.whole,)
            return
        q = width // 4
        parts = [(0, rows, base + i * q, q) for i in (self.g, self.gx, self.gy, self.gd)]
        self.ranges = tuple(parts[:3]) + tuple(self.half(parts[3], i) for i in range(2))

    def half(self, part, i):
        row, rows, col, cols = part
        return (row, rows, col + i * (cols // 2), cols // 2)

    def at(self, ref, row, rows, col, cols):
        row = row if isinstance(row, int) else pl.multiple_of(row, 16)
        col = col if isinstance(col, int) else pl.multiple_of(col, 128)
        return ref.at[pl.ds(row, rows), pl.ds(col, cols)]

    def copy(self, zz, core, part, s, r, dev, own=False):
        place = self.at(self.buf.at[zz * 2 + core], *part)
        src = self.at(self.own, *part) if own else place
        return pltpu.make_async_remote_copy(
            src_ref=src,
            dst_ref=place,
            send_sem=self.send.at[s, zz],
            recv_sem=self.recv.at[r, zz],
            device_id=dev,
            device_id_type=MESH,
        )

    def dev_z(self, zz):
        return (self.g, zz * 2 + self.c)

    @property
    def sibling(self):
        return (self.g, self.z * 2 + 1 - self.c)

    def up(self, zz, own=False):
        return self.copy(zz, self.c, self.ranges[0], 0, 0, self.dev_z(self.z + 1), own)

    def down(self, zz, own=False):
        return self.copy(zz, self.c, self.ranges[0], 1 if own else 0, 0, self.dev_z(self.z - 1), own)

    def to_x(self, zz):
        return self.copy(zz, self.c, self.ranges[0], 1, 1, (self.gx, self.t))

    def to_y(self, zz):
        return self.copy(zz, self.c, self.ranges[0], 2, 2, (self.gy, self.t))

    def on_y(self, zz):
        return self.copy(zz, self.c, self.half(self.ranges[1], 0), 3, 3, (self.gy, self.t))

    def on_x(self, zz):
        return self.copy(zz, self.c, self.half(self.ranges[2], 1), 4, 4, (self.gx, self.t))

    def across(self, zz, kind):
        return self.copy(zz, self.c, self.ranges[kind], 5 + kind, 5 + kind, self.sibling)

    def across_own(self):
        return self.copy(self.z, self.c, self.whole, 5, 5, self.sibling, True)

    def wait_recv(self, zz, kind):
        self.copy(zz, self.c, self.ranges[kind], kind, kind, self.sibling).wait_recv()

    def start(self):
        @pl.when(self.z + 1 < self.nz)
        def _():
            self.up(self.z, True).start()

        @pl.when(self.z > 0)
        def _():
            self.down(self.z, True).start()

        self.across_own().start()

    def arrive(self, zz):
        self.wait_recv(zz, 0)

        @pl.when((zz < self.z) & (self.z + 1 < self.nz))
        def _():
            self.up(zz).start()

        @pl.when((zz > self.z) & (self.z > 0))
        def _():
            self.down(zz).start()

        self.across(zz, 0).start()

    def spread(self, zz):
        self.to_x(zz).start()
        self.to_y(zz).start()

    def plane(self, zz):
        self.wait_recv(zz, 1)
        self.on_y(zz).start()
        self.across(zz, 1).start()
        self.wait_recv(zz, 2)
        self.on_x(zz).start()
        self.across(zz, 2).start()

    def diagonal(self, zz):
        for kind in (3, 4):
            self.wait_recv(zz, kind)
            self.across(zz, kind).start()

    def both(self, s, what):
        @pl.when((s >= 1) & (self.z - s >= 0))
        def _():
            what(self.z - s)

        @pl.when((s >= 1) & (self.z + s < self.nz))
        def _():
            what(self.z + s)

    def step(self, s):
        self.both(s - 1, self.plane)
        self.both(s - 2, self.diagonal)

    def finish(self):
        def settle(zz, carry):
            @pl.when(zz != self.z)
            def _():
                for kind in range(len(self.ranges)):
                    self.copy(
                        zz, 1 - self.c, self.ranges[kind], 5 + kind, 5 + kind, self.sibling
                    ).wait_recv()

            @pl.when(zz == self.z)
            def _():
                self.copy(zz, 1 - self.c, self.whole, 5, 5, self.sibling).wait_recv()

            return carry

        lax.fori_loop(0, self.nz, settle, 0)

    def sent(self):
        def settle(zz, carry):
            @pl.when(zz != self.z)
            def _():
                @pl.when((zz < self.z) & (self.z + 1 < self.nz))
                def _():
                    self.up(zz).wait_send()

                @pl.when((zz > self.z) & (self.z > 0))
                def _():
                    self.down(zz).wait_send()

                if self.split:
                    self.to_x(zz).wait_send()
                    self.to_y(zz).wait_send()
                    self.on_y(zz).wait_send()
                    self.on_x(zz).wait_send()
                for kind in range(len(self.ranges)):
                    self.across(zz, kind).wait_send()

            return carry

        lax.fori_loop(0, self.nz, settle, 0)

        @pl.when(self.z + 1 < self.nz)
        def _():
            self.up(self.z, True).wait_send()

        @pl.when(self.z > 0)
        def _():
            self.down(self.z, True).wait_send()

        self.across_own().wait_send()


def kernel(
    nt, ng,
    owner_ref, freq_ref, hidden_ref, ids_ref, prefix_ref, ngain_ref, qgain_ref, kgain_ref,
    wq_ref, wo_ref,
    out_ref, key_ref, value_ref,
    wq, wo, pall, psel, kv, ids_buf, normed, queries, attended, bias,
    k_send, k_recv,
    q_send, q_recv, o_send, o_recv, p_send, p_recv, pa_send, pa_recv,
    id_send, id_recv, kv_send, kv_recv,
):
    g, t = lax.axis_index("grp"), lax.axis_index("tok")
    nz = nt // 2
    z, c = t // 2, t % 2
    rows = hidden_ref.shape[1]
    head = qgain_ref.shape[1]
    kvw = key_ref.shape[2]
    kv_heads = kvw // head
    qkvw = wq.shape[2]
    qw = qkvw - 2 * kvw
    ratio = (qw // head) // kv_heads
    depth = wq.shape[0] * wq.shape[1]

    barrier = pltpu.get_barrier_semaphore()

    def greet_tok(k, carry):
        pl.semaphore_signal(
            barrier, inc=1, device_id=(g, (t + k) % nt), device_id_type=MESH
        )
        return carry

    lax.fori_loop(1, nt, greet_tok, 0)
    for k in range(1, ng):
        pl.semaphore_signal(
            barrier, inc=1, device_id=((g + k) % ng, t), device_id_type=MESH
        )
    ids = ids_ref[...]
    ids_buf[0] = jnp.broadcast_to(ids, ids_buf.shape[1:])
    for back in range(1, REACH + 1):
        @pl.when(t < back)
        def _():
            ids_buf[back] = jnp.full(ids_buf.shape[1:], -1, jnp.int32)
            kv[back] = jnp.zeros(kv.shape[1:], kv.dtype)
    pl.semaphore_wait(barrier, nt - 1 + ng - 1)

    kg = Gather(wq_ref, wq, k_send, k_recv, nz, True, qw, 2 * kvw)
    qg = Gather(wq_ref, wq, q_send, q_recv, nz, True, 0, qw)
    og = Gather(wo_ref, wo, o_send, o_recv, nz, True)
    pg = Gather(psel.at[t], psel, p_send, p_recv, nz, False)

    def id_copy(back):
        return pltpu.make_async_remote_copy(
            src_ref=ids_buf.at[0], dst_ref=ids_buf.at[back],
            send_sem=id_send.at[back], recv_sem=id_recv.at[back],
            device_id=(g, (t + back) % nt), device_id_type=MESH,
        )

    for back in range(1, REACH + 1):
        @pl.when(t + back < nt)
        def _():
            id_copy(back).start()

    def prefix_copy(k):
        return pltpu.make_async_remote_copy(
            src_ref=prefix_ref.at[0], dst_ref=pall.at[g],
            send_sem=pa_send.at[k], recv_sem=pa_recv.at[k],
            device_id=((g + k) % ng, t), device_id_type=MESH,
        )

    def prefix_got(k):
        return pltpu.make_async_remote_copy(
            src_ref=prefix_ref.at[0], dst_ref=pall.at[(g + ng - k) % ng],
            send_sem=pa_send.at[k], recv_sem=pa_recv.at[k],
            device_id=((g + k) % ng, t), device_id_type=MESH,
        )

    for k in range(1, ng):
        prefix_copy(k).start()
    kg.start()

    wq[t] = wq_ref[...]
    wo[t] = wo_ref[...]
    pall[g] = prefix_ref[0]

    def norm_rows(i, carry):
        at = pl.ds(pl.multiple_of(i * 64, 64), 64)
        x = hidden_ref[0, at, :].astype(jnp.float32)
        x = x * lax.rsqrt(jnp.mean(x * x, axis=-1, keepdims=True) + epsilon)
        normed[at, :] = (x * ngain_ref[...].astype(jnp.float32).reshape(1, -1)).astype(jnp.bfloat16)
        return carry

    lax.fori_loop(0, rows // 64, norm_rows, 0)

    for k in range(1, ng):
        prefix_got(k).wait_recv()
    psel[t] = pall[owner_ref[g]]

    for back in range(1, REACH + 1):
        @pl.when(t >= back)
        def _():
            id_copy(back).wait_recv()
    column = jnp.transpose(
        jnp.broadcast_to(ids.astype(jnp.float32), (128, rows)), (1, 0)
    )[:, :1]
    here = lax.broadcasted_iota(jnp.int32, (rows, rows), 0)
    there = lax.broadcasted_iota(jnp.int32, (rows, rows), 1)
    count = jnp.zeros((rows, 1), jnp.float32)
    for back in range(REACH + 1):
        allowed = column == ids_buf[back, 0:1, :].astype(jnp.float32)
        if back == 0:
            allowed = allowed & (there <= here)
        count += jnp.sum(jnp.where(allowed, 1.0, 0.0), axis=-1, keepdims=True)
        bias[back] = jnp.where(allowed, 0.0, floor_score)
    prefix_len = psel.shape[0] * psel.shape[1]
    position = count + (prefix_len - 1.0)
    angles = position * freq_ref[...]
    cosine = jnp.cos(angles)
    lane = lax.broadcasted_iota(jnp.int32, (rows, head), 1)
    sine = jnp.sin(angles)
    sine = jnp.where(lane < head // 2, -sine, sine)

    def first(s, carry):
        kg.both(s, kg.arrive)
        kg.both(s, kg.spread)
        kg.step(s)
        return carry

    lax.fori_loop(1, nz, first, 0)
    qg.start()
    pg.start()

    def second(s, carry):
        qg.both(s, qg.arrive)
        kg.step(nz - 1 + s)
        qg.both(s, qg.spread)
        return carry

    lax.fori_loop(1, nz, second, 0)
    og.start()
    kg.finish()

    def project(j):
        at = pl.ds(pl.multiple_of(j * BLOCK, BLOCK), BLOCK)
        w = wq[:, :, at].reshape(depth, BLOCK)
        return jnp.dot(normed[...], w, preferred_element_type=jnp.float32)

    def turned(block, gain):
        parts = []
        for i in range(BLOCK // head):
            a = block[:, i * head:(i + 1) * head]
            a = a * lax.rsqrt(jnp.mean(a * a, axis=-1, keepdims=True) + epsilon)
            a = a * gain
            a = a * cosine + pltpu.roll(a, head // 2, 1) * sine
            parts.append(a.astype(jnp.bfloat16))
        return jnp.concatenate(parts, axis=1)

    def key_block(j, carry):
        at = pl.ds(pl.multiple_of(j * BLOCK, BLOCK), BLOCK)
        made = turned(project(qw // BLOCK + j), kgain_ref[...].astype(jnp.float32))
        kv[0, :, at] = made
        key_ref[0, :, at] = made
        return carry

    def value_block(j, carry):
        made = project((qw + kvw) // BLOCK + j).astype(jnp.bfloat16)
        kv[0, :, pl.ds(pl.multiple_of(kvw + j * BLOCK, BLOCK), BLOCK)] = made
        value_ref[0, :, pl.ds(pl.multiple_of(j * BLOCK, BLOCK), BLOCK)] = made
        return carry

    def query_block(j, carry):
        at = pl.ds(pl.multiple_of(j * BLOCK, BLOCK), BLOCK)
        queries[:, at] = turned(project(j), qgain_ref[...].astype(jnp.float32))
        return carry

    def out_arrive(s, carry):
        og.both(s, og.arrive)
        return carry

    lax.fori_loop(0, kvw // BLOCK, key_block, 0)
    out_arrive(1, 0)
    lax.fori_loop(0, kvw // BLOCK, value_block, 0)

    def kv_copy(src, dst, dev):
        return pltpu.make_async_remote_copy(
            src_ref=kv.at[src], dst_ref=kv.at[dst],
            send_sem=kv_send.at[dst], recv_sem=kv_recv.at[dst],
            device_id=(g, dev), device_id_type=MESH,
        )

    to_next = kv_copy(0, 2, (t + 2) % nt)
    beside = kv_copy(0, 1, z * 2 + 1 - c)
    passed_on = kv_copy(2, 1, z * 2 + 1 - c)

    @pl.when(t + 2 < nt)
    def _():
        to_next.start()

    @pl.when(c == 0)
    def _():
        beside.start()

    def third(s, carry):
        pg.both(s, pg.arrive)
        qg.step(s + 1)
        return carry

    lax.fori_loop(1, nz, third, 0)
    lax.fori_loop(2, nz, out_arrive, 0)

    def out_spread(s, carry):
        og.both(s, og.spread)
        return carry

    lax.fori_loop(1, nz, out_spread, 0)
    qg.step(nz + 1)
    qg.finish()
    lax.fori_loop(0, qw // BLOCK, query_block, 0)
    pg.finish()

    def fourth(s, carry):
        og.step(s)
        return carry


    @pl.when(t >= 2)
    def _():
        to_next.wait_recv()

    @pl.when((c == 1) & (z > 0))
    def _():
        passed_on.start()

    @pl.when(t >= 1)
    def _():
        beside.wait_recv()

    factor = head ** (-0.5) * math.log2(math.e)
    dims = (((1,), (1,)), ((), ()))

    def attend(h, carry):
        kat = pl.ds(pl.multiple_of(h * head, head), head)
        vat = pl.ds(pl.multiple_of(kvw + h * head, head), head)
        q = jnp.concatenate(
            [
                queries[:, pl.ds(pl.multiple_of((h * ratio + r) * head, head), head)]
                for r in range(ratio)
            ],
            axis=0,
        )
        keys = [psel[:, :, kat].reshape(prefix_len, head)]
        values = [psel[:, :, vat].reshape(prefix_len, head)]
        for back in range(REACH + 1):
            keys.append(kv[back, :, kat])
            values.append(kv[back, :, vat])
        scores = []
        for i, k in enumerate(keys):
            s = lax.dot_general(q, k, dims, preferred_element_type=jnp.float32)
            if i:
                s = (s.reshape(ratio, rows, rows) + bias[i - 1][None]).reshape(ratio * rows, rows)
            scores.append(s)
        top = functools.reduce(
            jnp.maximum, [jnp.max(s, axis=-1, keepdims=True) for s in scores]
        )
        total, mixed = 0.0, 0.0
        for s, v in zip(scores, values):
            p = jnp.exp2((s - top) * factor)
            total += jnp.sum(p, axis=-1, keepdims=True)
            mixed += jnp.dot(p.astype(jnp.bfloat16), v, preferred_element_type=jnp.float32)
        mixed = (mixed / total).astype(jnp.bfloat16)
        for r in range(ratio):
            attended[:, pl.ds(pl.multiple_of((h * ratio + r) * head, head), head)] = mixed[
                r * rows:(r + 1) * rows
            ]

        lax.fori_loop(2 + h * per, jnp.minimum(2 + (h + 1) * per, nz + 2), fourth, 0)
        return carry

    per = -(-nz // kv_heads)
    lax.fori_loop(0, kv_heads, attend, 0)
    og.finish()

    def out_block(j, carry):
        at = pl.ds(pl.multiple_of(j * BLOCK, BLOCK), BLOCK)
        w = wo[:, :, at].reshape(qw, BLOCK)
        out_ref[0, :, at] = jnp.dot(
            attended[...], w, preferred_element_type=jnp.float32
        ).astype(jnp.bfloat16)
        return carry

    lax.fori_loop(0, out_ref.shape[2] // BLOCK, out_block, 0)

    for one in (kg, qg, og, pg):
        one.sent()
    for k in range(1, ng):
        prefix_copy(k).wait_send()
    for back in range(1, REACH + 1):
        @pl.when(t + back < nt)
        def _():
            id_copy(back).wait_send()

    @pl.when(t + 2 < nt)
    def _():
        to_next.wait_send()

    @pl.when(c == 0)
    def _():
        beside.wait_send()

    @pl.when((c == 1) & (z > 0))
    def _():
        passed_on.wait_send()


def place(*refs):
    count = len(refs) // 2
    for src, dst in zip(refs[:count], refs[count:]):
        dst[...] = src[...]


def per_device(
    nt, ng,
    hidden_in, doc_ids, prefix_kv, prefix_owner, norm_gain, query_gain, key_norm_gain, w_qkv, w_out
):
    rows, width = hidden_in.shape[1:]
    head = query_gain.shape[0]
    kvw = prefix_kv.shape[2] // 2
    pre = prefix_kv.shape[1]
    qkvw = w_qkv.shape[1]
    qw = qkvw - 2 * kvw
    nz = nt // 2
    half = head // 2
    freqs = np.float32(theta_base) ** (-np.arange(half, dtype=np.float32) / np.float32(half))
    freqs = np.concatenate([freqs, freqs]).astype(np.float32)[None]
    bf = jnp.bfloat16
    vm = pl.BlockSpec(memory_space=pltpu.VMEM)
    dma = pltpu.SemaphoreType.DMA
    made = pl.pallas_call(
        functools.partial(kernel, nt, ng),
        out_shape=(
            jax.ShapeDtypeStruct((1, rows, w_out.shape[1]), bf),
            jax.ShapeDtypeStruct((1, rows, kvw), bf),
            jax.ShapeDtypeStruct((1, rows, kvw), bf),
        ),
        in_specs=[pl.BlockSpec(memory_space=pltpu.SMEM)] + [vm] * 9,
        out_specs=(vm, vm, vm),
        scratch_shapes=[
            pltpu.VMEM((nt,) + w_qkv.shape, bf),
            pltpu.VMEM((nt,) + w_out.shape, bf),
            pltpu.VMEM((ng, pre, 2 * kvw), bf),
            pltpu.VMEM((nt, pre, 2 * kvw), bf),
            pltpu.VMEM((REACH + 1, rows, 2 * kvw), bf),
            pltpu.VMEM((REACH + 1, 8, rows), jnp.int32),
            pltpu.VMEM((rows, width), bf),
            pltpu.VMEM((rows, qw), bf),
            pltpu.VMEM((rows, qw), bf),
            pltpu.VMEM((REACH + 1, rows, rows), jnp.float32),
            dma((10, nz)), dma((10, nz)),
            dma((10, nz)), dma((10, nz)),
            dma((10, nz)), dma((10, nz)),
            dma((10, nz)), dma((10, nz)),
            dma((ng,)), dma((ng,)),
            dma((REACH + 1,)), dma((REACH + 1,)),
            dma((REACH + 1,)), dma((REACH + 1,)),
        ],
        compiler_params=pltpu.CompilerParams(
            collective_id=0, has_side_effects=True, vmem_limit_bytes=56 * 1024 * 1024
        ),
    )(
        prefix_owner, jnp.asarray(freqs), hidden_in, doc_ids, prefix_kv,
        norm_gain, query_gain[None], key_norm_gain[None], w_qkv, w_out,
    )
    parts = [
        pl.BlockSpec((1, rows // 4, x.shape[2]), lambda i: (0, i, 0)) for x in made
    ]
    return pl.pallas_call(
        place,
        grid=(4,),
        out_shape=tuple(jax.ShapeDtypeStruct(x.shape, x.dtype) for x in made),
        in_specs=parts,
        out_specs=tuple(parts),
        compiler_params=pltpu.CompilerParams(vmem_limit_bytes=63 * 1024 * 1024),
    )(*made)


def solution(mesh):
    return jax.shard_map(
        functools.partial(per_device, mesh.shape["tok"], mesh.shape["grp"]),
        mesh=mesh,
        in_specs=(
            P("grp", "tok", None),
            P("grp", "tok"),
            P("grp", "tok", None),
            P(),
            P(),
            P(),
            P(),
            P("tok", None),
            P("tok", None),
        ),
        out_specs=(P("grp", "tok", None), P("grp", "tok", None), P("grp", "tok", None)),
        check_vma=False,
    )
```

```python
import functools
import math

import jax
import jax.numpy as jnp
import numpy as np
from jax import lax
from jax.experimental import pallas as pl
from jax.experimental.pallas import tpu as pltpu
from jax.sharding import PartitionSpec as P

MESH = pl.DeviceIdType.MESH
epsilon = 1e-06
theta_base = 1000000.0
floor_score = -1e30
REACH = 2
BLOCK = 256


class Gather:
    def __init__(self, own, buf, send, recv, nz, split, base=0, width=None):
        self.own, self.buf, self.send, self.recv = own, buf, send, recv
        self.nz, self.split = nz, split
        g, t = lax.axis_index("grp"), lax.axis_index("tok")
        self.g, self.t = g, t
        self.z, self.c = t // 2, t % 2
        self.gx = g + 1 - 2 * (g % 2)
        self.gy = (g + 2) % 4
        self.gd = (self.gx + 2) % 4
        width = buf.shape[2] if width is None else width
        rows = buf.shape[1]
        self.whole = (0, rows, base, width)
        if not split:
            self.ranges = (self.whole,)
            return
        q = width // 4
        parts = [(0, rows, base + i * q, q) for i in (self.g, self.gx, self.gy, self.gd)]
        self.ranges = tuple(parts[:3]) + tuple(self.half(parts[3], i) for i in range(2))

    def half(self, part, i):
        row, rows, col, cols = part
        return (row, rows, col + i * (cols // 2), cols // 2)

    def at(self, ref, row, rows, col, cols):
        row = row if isinstance(row, int) else pl.multiple_of(row, 16)
        col = col if isinstance(col, int) else pl.multiple_of(col, 128)
        return ref.at[pl.ds(row, rows), pl.ds(col, cols)]

    def copy(self, zz, core, part, s, r, dev, own=False):
        place = self.at(self.buf.at[zz * 2 + core], *part)
        src = self.at(self.own, *part) if own else place
        return pltpu.make_async_remote_copy(
            src_ref=src,
            dst_ref=place,
            send_sem=self.send.at[s, zz],
            recv_sem=self.recv.at[r, zz],
            device_id=dev,
            device_id_type=MESH,
        )

    def dev_z(self, zz):
        return (self.g, zz * 2 + self.c)

    @property
    def sibling(self):
        return (self.g, self.z * 2 + 1 - self.c)

    def up(self, zz, own=False):
        return self.copy(zz, self.c, self.ranges[0], 0, 0, self.dev_z(self.z + 1), own)

    def down(self, zz, own=False):
        return self.copy(zz, self.c, self.ranges[0], 1 if own else 0, 0, self.dev_z(self.z - 1), own)

    def to_x(self, zz):
        return self.copy(zz, self.c, self.ranges[0], 1, 1, (self.gx, self.t))

    def to_y(self, zz):
        return self.copy(zz, self.c, self.ranges[0], 2, 2, (self.gy, self.t))

    def on_y(self, zz):
        return self.copy(zz, self.c, self.half(self.ranges[1], 0), 3, 3, (self.gy, self.t))

    def on_x(self, zz):
        return self.copy(zz, self.c, self.half(self.ranges[2], 1), 4, 4, (self.gx, self.t))

    def across(self, zz, kind):
        return self.copy(zz, self.c, self.ranges[kind], 5 + kind, 5 + kind, self.sibling)

    def across_own(self):
        return self.copy(self.z, self.c, self.whole, 5, 5, self.sibling, True)

    def wait_recv(self, zz, kind):
        self.copy(zz, self.c, self.ranges[kind], kind, kind, self.sibling).wait_recv()

    def start(self):
        @pl.when(self.z + 1 < self.nz)
        def _():
            self.up(self.z, True).start()

        @pl.when(self.z > 0)
        def _():
            self.down(self.z, True).start()

        self.across_own().start()

    def arrive(self, zz):
        self.wait_recv(zz, 0)

        @pl.when((zz < self.z) & (self.z + 1 < self.nz))
        def _():
            self.up(zz).start()

        @pl.when((zz > self.z) & (self.z > 0))
        def _():
            self.down(zz).start()

        self.across(zz, 0).start()

    def spread(self, zz):
        self.to_x(zz).start()
        self.to_y(zz).start()

    def plane(self, zz):
        self.wait_recv(zz, 1)
        self.on_y(zz).start()
        self.across(zz, 1).start()
        self.wait_recv(zz, 2)
        self.on_x(zz).start()
        self.across(zz, 2).start()

    def diagonal(self, zz):
        for kind in (3, 4):
            self.wait_recv(zz, kind)
            self.across(zz, kind).start()

    def both(self, s, what):
        @pl.when((s >= 1) & (self.z - s >= 0))
        def _():
            what(self.z - s)

        @pl.when((s >= 1) & (self.z + s < self.nz))
        def _():
            what(self.z + s)

    def step(self, s):
        self.both(s - 1, self.plane)
        self.both(s - 2, self.diagonal)

    def finish(self):
        def settle(zz, carry):
            @pl.when(zz != self.z)
            def _():
                for kind in range(len(self.ranges)):
                    self.copy(
                        zz, 1 - self.c, self.ranges[kind], 5 + kind, 5 + kind, self.sibling
                    ).wait_recv()

            @pl.when(zz == self.z)
            def _():
                self.copy(zz, 1 - self.c, self.whole, 5, 5, self.sibling).wait_recv()

            return carry

        lax.fori_loop(0, self.nz, settle, 0)

    def sent(self):
        def settle(zz, carry):
            @pl.when(zz != self.z)
            def _():
                @pl.when((zz < self.z) & (self.z + 1 < self.nz))
                def _():
                    self.up(zz).wait_send()

                @pl.when((zz > self.z) & (self.z > 0))
                def _():
                    self.down(zz).wait_send()

                if self.split:
                    self.to_x(zz).wait_send()
                    self.to_y(zz).wait_send()
                    self.on_y(zz).wait_send()
                    self.on_x(zz).wait_send()
                for kind in range(len(self.ranges)):
                    self.across(zz, kind).wait_send()

            return carry

        lax.fori_loop(0, self.nz, settle, 0)

        @pl.when(self.z + 1 < self.nz)
        def _():
            self.up(self.z, True).wait_send()

        @pl.when(self.z > 0)
        def _():
            self.down(self.z, True).wait_send()

        self.across_own().wait_send()


def kernel(
    nt, ng,
    owner_ref, freq_ref, hidden_ref, ids_ref, prefix_ref, ngain_ref, qgain_ref, kgain_ref,
    wq_ref, wo_ref,
    out_ref, key_ref, value_ref,
    wq, wo, pall, psel, kv, ids_buf, normed, queries, attended, bias,
    k_send, k_recv,
    q_send, q_recv, o_send, o_recv, p_send, p_recv, pa_send, pa_recv,
    id_send, id_recv, kv_send, kv_recv,
):
    g, t = lax.axis_index("grp"), lax.axis_index("tok")
    nz = nt // 2
    z, c = t // 2, t % 2
    rows = hidden_ref.shape[1]
    head = qgain_ref.shape[1]
    kvw = key_ref.shape[2]
    kv_heads = kvw // head
    qkvw = wq.shape[2]
    qw = qkvw - 2 * kvw
    ratio = (qw // head) // kv_heads
    depth = wq.shape[0] * wq.shape[1]

    barrier = pltpu.get_barrier_semaphore()

    def greet_tok(k, carry):
        pl.semaphore_signal(
            barrier, inc=1, device_id=(g, (t + k) % nt), device_id_type=MESH
        )
        return carry

    lax.fori_loop(1, nt, greet_tok, 0)
    for k in range(1, ng):
        pl.semaphore_signal(
            barrier, inc=1, device_id=((g + k) % ng, t), device_id_type=MESH
        )
    ids = ids_ref[...]
    ids_buf[0] = jnp.broadcast_to(ids, ids_buf.shape[1:])
    for back in range(1, REACH + 1):
        @pl.when(t < back)
        def _():
            ids_buf[back] = jnp.full(ids_buf.shape[1:], -1, jnp.int32)
            kv[back] = jnp.zeros(kv.shape[1:], kv.dtype)
    pl.semaphore_wait(barrier, nt - 1 + ng - 1)

    kg = Gather(wq_ref, wq, k_send, k_recv, nz, True, qw, 2 * kvw)
    qg = Gather(wq_ref, wq, q_send, q_recv, nz, True, 0, qw)
    og = Gather(wo_ref, wo, o_send, o_recv, nz, True)
    pg = Gather(psel.at[t], psel, p_send, p_recv, nz, False)

    def id_copy(back):
        return pltpu.make_async_remote_copy(
            src_ref=ids_buf.at[0], dst_ref=ids_buf.at[back],
            send_sem=id_send.at[back], recv_sem=id_recv.at[back],
            device_id=(g, (t + back) % nt), device_id_type=MESH,
        )

    for back in range(1, REACH + 1):
        @pl.when(t + back < nt)
        def _():
            id_copy(back).start()

    def prefix_copy(k):
        return pltpu.make_async_remote_copy(
            src_ref=prefix_ref.at[0], dst_ref=pall.at[g],
            send_sem=pa_send.at[k], recv_sem=pa_recv.at[k],
            device_id=((g + k) % ng, t), device_id_type=MESH,
        )

    def prefix_got(k):
        return pltpu.make_async_remote_copy(
            src_ref=prefix_ref.at[0], dst_ref=pall.at[(g + ng - k) % ng],
            send_sem=pa_send.at[k], recv_sem=pa_recv.at[k],
            device_id=((g + k) % ng, t), device_id_type=MESH,
        )

    for k in range(1, ng):
        prefix_copy(k).start()
    kg.start()

    wq[t] = wq_ref[...]
    wo[t] = wo_ref[...]
    pall[g] = prefix_ref[0]

    def norm_rows(i, carry):
        at = pl.ds(pl.multiple_of(i * 64, 64), 64)
        x = hidden_ref[0, at, :].astype(jnp.float32)
        x = x * lax.rsqrt(jnp.mean(x * x, axis=-1, keepdims=True) + epsilon)
        normed[at, :] = (x * ngain_ref[...].astype(jnp.float32).reshape(1, -1)).astype(jnp.bfloat16)
        return carry

    lax.fori_loop(0, rows // 64, norm_rows, 0)

    for k in range(1, ng):
        prefix_got(k).wait_recv()
    psel[t] = pall[owner_ref[g]]

    for back in range(1, REACH + 1):
        @pl.when(t >= back)
        def _():
            id_copy(back).wait_recv()
    column = jnp.transpose(
        jnp.broadcast_to(ids.astype(jnp.float32), (128, rows)), (1, 0)
    )[:, :1]
    here = lax.broadcasted_iota(jnp.int32, (rows, rows), 0)
    there = lax.broadcasted_iota(jnp.int32, (rows, rows), 1)
    count = jnp.zeros((rows, 1), jnp.float32)
    for back in range(REACH + 1):
        allowed = column == ids_buf[back, 0:1, :].astype(jnp.float32)
        if back == 0:
            allowed = allowed & (there <= here)
        count += jnp.sum(jnp.where(allowed, 1.0, 0.0), axis=-1, keepdims=True)
        bias[back] = jnp.where(allowed, 0.0, floor_score)
    prefix_len = psel.shape[0] * psel.shape[1]
    position = count + (prefix_len - 1.0)
    angles = position * freq_ref[...]
    cosine = jnp.cos(angles)
    lane = lax.broadcasted_iota(jnp.int32, (rows, head), 1)
    sine = jnp.sin(angles)
    sine = jnp.where(lane < head // 2, -sine, sine)

    def first(s, carry):
        kg.both(s, kg.arrive)
        kg.both(s, kg.spread)
        kg.step(s)
        return carry

    lax.fori_loop(1, nz, first, 0)
    qg.start()
    pg.start()

    def second(s, carry):
        qg.both(s, qg.arrive)
        kg.step(nz - 1 + s)
        qg.both(s, qg.spread)
        return carry

    lax.fori_loop(1, nz, second, 0)
    og.start()
    kg.finish()

    def project(j):
        at = pl.ds(pl.multiple_of(j * BLOCK, BLOCK), BLOCK)
        w = wq[:, :, at].reshape(depth, BLOCK)
        return jnp.dot(normed[...], w, preferred_element_type=jnp.float32)

    def turned(block, gain):
        parts = []
        for i in range(BLOCK // head):
            a = block[:, i * head:(i + 1) * head]
            a = a * lax.rsqrt(jnp.mean(a * a, axis=-1, keepdims=True) + epsilon)
            a = a * gain
            a = a * cosine + pltpu.roll(a, head // 2, 1) * sine
            parts.append(a.astype(jnp.bfloat16))
        return jnp.concatenate(parts, axis=1)

    def key_block(j, carry):
        at = pl.ds(pl.multiple_of(j * BLOCK, BLOCK), BLOCK)
        made = turned(project(qw // BLOCK + j), kgain_ref[...].astype(jnp.float32))
        kv[0, :, at] = made
        key_ref[0, :, at] = made
        return carry

    def value_block(j, carry):
        made = project((qw + kvw) // BLOCK + j).astype(jnp.bfloat16)
        kv[0, :, pl.ds(pl.multiple_of(kvw + j * BLOCK, BLOCK), BLOCK)] = made
        value_ref[0, :, pl.ds(pl.multiple_of(j * BLOCK, BLOCK), BLOCK)] = made
        return carry

    def query_block(j, carry):
        at = pl.ds(pl.multiple_of(j * BLOCK, BLOCK), BLOCK)
        queries[:, at] = turned(project(j), qgain_ref[...].astype(jnp.float32))
        return carry

    def out_arrive(s, carry):
        og.both(s, og.arrive)
        return carry

    lax.fori_loop(0, kvw // BLOCK, key_block, 0)
    out_arrive(1, 0)
    lax.fori_loop(0, kvw // BLOCK, value_block, 0)

    def kv_copy(src, dst, dev):
        return pltpu.make_async_remote_copy(
            src_ref=kv.at[src], dst_ref=kv.at[dst],
            send_sem=kv_send.at[dst], recv_sem=kv_recv.at[dst],
            device_id=(g, dev), device_id_type=MESH,
        )

    to_next = kv_copy(0, 2, (t + 2) % nt)
    beside = kv_copy(0, 1, z * 2 + 1 - c)
    passed_on = kv_copy(2, 1, z * 2 + 1 - c)

    @pl.when(t + 2 < nt)
    def _():
        to_next.start()

    @pl.when(c == 0)
    def _():
        beside.start()

    def third(s, carry):
        pg.both(s, pg.arrive)
        qg.step(s + 1)
        return carry

    lax.fori_loop(1, nz, third, 0)
    lax.fori_loop(2, nz, out_arrive, 0)

    def out_spread(s, carry):
        og.both(s, og.spread)
        return carry

    lax.fori_loop(1, nz, out_spread, 0)
    qg.step(nz + 1)
    qg.finish()
    lax.fori_loop(0, qw // BLOCK, query_block, 0)
    pg.finish()

    def fourth(s, carry):
        og.step(s)
        return carry


    for one in (kg, qg, pg):
        one.sent()
    for k in range(1, ng):
        prefix_copy(k).wait_send()
    for back in range(1, REACH + 1):
        @pl.when(t + back < nt)
        def _():
            id_copy(back).wait_send()

    @pl.when(t >= 2)
    def _():
        to_next.wait_recv()

    @pl.when((c == 1) & (z > 0))
    def _():
        passed_on.start()

    @pl.when(t >= 1)
    def _():
        beside.wait_recv()

    factor = head ** (-0.5) * math.log2(math.e)
    dims = (((1,), (1,)), ((), ()))

    def attend(h, carry):
        kat = pl.ds(pl.multiple_of(h * head, head), head)
        vat = pl.ds(pl.multiple_of(kvw + h * head, head), head)
        q = jnp.concatenate(
            [
                queries[:, pl.ds(pl.multiple_of((h * ratio + r) * head, head), head)]
                for r in range(ratio)
            ],
            axis=0,
        )
        keys = [psel[:, :, kat].reshape(prefix_len, head)]
        values = [psel[:, :, vat].reshape(prefix_len, head)]
        for back in range(REACH + 1):
            keys.append(kv[back, :, kat])
            values.append(kv[back, :, vat])
        scores = []
        for i, k in enumerate(keys):
            s = lax.dot_general(q, k, dims, preferred_element_type=jnp.float32)
            if i:
                s = (s.reshape(ratio, rows, rows) + bias[i - 1][None]).reshape(ratio * rows, rows)
            scores.append(s)
        top = functools.reduce(
            jnp.maximum, [jnp.max(s, axis=-1, keepdims=True) for s in scores]
        )
        total, mixed = 0.0, 0.0
        for s, v in zip(scores, values):
            p = jnp.exp2((s - top) * factor)
            total += jnp.sum(p, axis=-1, keepdims=True)
            mixed += jnp.dot(p.astype(jnp.bfloat16), v, preferred_element_type=jnp.float32)
        mixed = (mixed / total).astype(jnp.bfloat16)
        for r in range(ratio):
            attended[:, pl.ds(pl.multiple_of((h * ratio + r) * head, head), head)] = mixed[
                r * rows:(r + 1) * rows
            ]

        lax.fori_loop(2 + h * per, jnp.minimum(2 + (h + 1) * per, nz + 2), fourth, 0)
        return carry

    per = -(-nz // kv_heads)
    lax.fori_loop(0, kv_heads, attend, 0)
    og.finish()

    def out_block(j, carry):
        at = pl.ds(pl.multiple_of(j * BLOCK, BLOCK), BLOCK)
        w = wo[:, :, at].reshape(qw, BLOCK)
        out_ref[0, :, at] = jnp.dot(
            attended[...], w, preferred_element_type=jnp.float32
        ).astype(jnp.bfloat16)
        return carry

    lax.fori_loop(0, out_ref.shape[2] // BLOCK, out_block, 0)

    og.sent()

    @pl.when(t + 2 < nt)
    def _():
        to_next.wait_send()

    @pl.when(c == 0)
    def _():
        beside.wait_send()

    @pl.when((c == 1) & (z > 0))
    def _():
        passed_on.wait_send()


def place(*refs):
    count = (len(refs) - 1) // 2
    sems = refs[-1]
    copies = [
        pltpu.make_async_copy(refs[i], refs[count + i], sems.at[i]) for i in range(count)
    ]
    for one in copies:
        one.start()
    for one in copies:
        one.wait()


def per_device(
    nt, ng,
    hidden_in, doc_ids, prefix_kv, prefix_owner, norm_gain, query_gain, key_norm_gain, w_qkv, w_out
):
    rows, width = hidden_in.shape[1:]
    head = query_gain.shape[0]
    kvw = prefix_kv.shape[2] // 2
    pre = prefix_kv.shape[1]
    qkvw = w_qkv.shape[1]
    qw = qkvw - 2 * kvw
    nz = nt // 2
    half = head // 2
    freqs = np.float32(theta_base) ** (-np.arange(half, dtype=np.float32) / np.float32(half))
    freqs = np.concatenate([freqs, freqs]).astype(np.float32)[None]
    bf = jnp.bfloat16
    vm = pl.BlockSpec(memory_space=pltpu.VMEM)
    dma = pltpu.SemaphoreType.DMA
    made = pl.pallas_call(
        functools.partial(kernel, nt, ng),
        out_shape=(
            pltpu.VMEM((1, rows, w_out.shape[1]), bf),
            pltpu.VMEM((1, rows, kvw), bf),
            pltpu.VMEM((1, rows, kvw), bf),
        ),
        in_specs=[pl.BlockSpec(memory_space=pltpu.SMEM)] + [vm] * 9,
        out_specs=(vm, vm, vm),
        scratch_shapes=[
            pltpu.VMEM((nt,) + w_qkv.shape, bf),
            pltpu.VMEM((nt,) + w_out.shape, bf),
            pltpu.VMEM((ng, pre, 2 * kvw), bf),
            pltpu.VMEM((nt, pre, 2 * kvw), bf),
            pltpu.VMEM((REACH + 1, rows, 2 * kvw), bf),
            pltpu.VMEM((REACH + 1, 8, rows), jnp.int32),
            pltpu.VMEM((rows, width), bf),
            pltpu.VMEM((rows, qw), bf),
            pltpu.VMEM((rows, qw), bf),
            pltpu.VMEM((REACH + 1, rows, rows), jnp.float32),
            dma((10, nz)), dma((10, nz)),
            dma((10, nz)), dma((10, nz)),
            dma((10, nz)), dma((10, nz)),
            dma((10, nz)), dma((10, nz)),
            dma((ng,)), dma((ng,)),
            dma((REACH + 1,)), dma((REACH + 1,)),
            dma((REACH + 1,)), dma((REACH + 1,)),
        ],
        compiler_params=pltpu.CompilerParams(
            collective_id=0, has_side_effects=True, vmem_limit_bytes=56 * 1024 * 1024
        ),
    )(
        prefix_owner, jnp.asarray(freqs), hidden_in, doc_ids, prefix_kv,
        norm_gain, query_gain[None], key_norm_gain[None], w_qkv, w_out,
    )
    return pl.pallas_call(
        place,
        out_shape=tuple(jax.ShapeDtypeStruct(x.shape, x.dtype) for x in made),
        in_specs=[vm] * len(made),
        out_specs=(pl.BlockSpec(memory_space=pl.ANY),) * len(made),
        scratch_shapes=[dma((len(made),))],
    )(*made)


def solution(mesh):
    return jax.shard_map(
        functools.partial(per_device, mesh.shape["tok"], mesh.shape["grp"]),
        mesh=mesh,
        in_specs=(
            P("grp", "tok", None),
            P("grp", "tok"),
            P("grp", "tok", None),
            P(),
            P(),
            P(),
            P(),
            P("tok", None),
            P("tok", None),
        ),
        out_specs=(P("grp", "tok", None), P("grp", "tok", None), P("grp", "tok", None)),
        check_vma=False,
    )
```

```python
import functools
import math

import jax
import jax.numpy as jnp
import numpy as np
from jax import lax
from jax.experimental import pallas as pl
from jax.experimental.pallas import tpu as pltpu
from jax.sharding import PartitionSpec as P

MESH = pl.DeviceIdType.MESH
epsilon = 1e-06
theta_base = 1000000.0
floor_score = -1e30
REACH = 2
BLOCK = 256


class Gather:
    def __init__(self, own, buf, send, recv, nz, split, base=0, width=None):
        self.own, self.buf, self.send, self.recv = own, buf, send, recv
        self.nz, self.split = nz, split
        g, t = lax.axis_index("grp"), lax.axis_index("tok")
        self.g, self.t = g, t
        self.z, self.c = t // 2, t % 2
        self.gx = g + 1 - 2 * (g % 2)
        self.gy = (g + 2) % 4
        self.gd = (self.gx + 2) % 4
        width = buf.shape[2] if width is None else width
        rows = buf.shape[1]
        self.whole = (0, rows, base, width)
        if not split:
            self.ranges = (self.whole,)
            return
        q = width // 4
        parts = [(0, rows, base + i * q, q) for i in (self.g, self.gx, self.gy, self.gd)]
        self.ranges = tuple(parts[:3]) + tuple(self.half(parts[3], i) for i in range(2))

    def half(self, part, i):
        row, rows, col, cols = part
        return (row, rows, col + i * (cols // 2), cols // 2)

    def at(self, ref, row, rows, col, cols):
        row = row if isinstance(row, int) else pl.multiple_of(row, 16)
        col = col if isinstance(col, int) else pl.multiple_of(col, 128)
        return ref.at[pl.ds(row, rows), pl.ds(col, cols)]

    def copy(self, zz, core, part, s, r, dev, own=False):
        place = self.at(self.buf.at[zz * 2 + core], *part)
        src = self.at(self.own, *part) if own else place
        return pltpu.make_async_remote_copy(
            src_ref=src,
            dst_ref=place,
            send_sem=self.send.at[s, zz],
            recv_sem=self.recv.at[r, zz],
            device_id=dev,
            device_id_type=MESH,
        )

    def dev_z(self, zz):
        return (self.g, zz * 2 + self.c)

    @property
    def sibling(self):
        return (self.g, self.z * 2 + 1 - self.c)

    def up(self, zz, own=False):
        return self.copy(zz, self.c, self.ranges[0], 0, 0, self.dev_z(self.z + 1), own)

    def down(self, zz, own=False):
        return self.copy(zz, self.c, self.ranges[0], 1 if own else 0, 0, self.dev_z(self.z - 1), own)

    def to_x(self, zz):
        return self.copy(zz, self.c, self.ranges[0], 1, 1, (self.gx, self.t))

    def to_y(self, zz):
        return self.copy(zz, self.c, self.ranges[0], 2, 2, (self.gy, self.t))

    def on_y(self, zz):
        return self.copy(zz, self.c, self.half(self.ranges[1], 0), 3, 3, (self.gy, self.t))

    def on_x(self, zz):
        return self.copy(zz, self.c, self.half(self.ranges[2], 1), 4, 4, (self.gx, self.t))

    def across(self, zz, kind):
        return self.copy(zz, self.c, self.ranges[kind], 5 + kind, 5 + kind, self.sibling)

    def across_own(self):
        return self.copy(self.z, self.c, self.whole, 5, 5, self.sibling, True)

    def wait_recv(self, zz, kind):
        self.copy(zz, self.c, self.ranges[kind], kind, kind, self.sibling).wait_recv()

    def start(self):
        @pl.when(self.z + 1 < self.nz)
        def _():
            self.up(self.z, True).start()

        @pl.when(self.z > 0)
        def _():
            self.down(self.z, True).start()

        self.across_own().start()

    def arrive(self, zz):
        self.wait_recv(zz, 0)

        @pl.when((zz < self.z) & (self.z + 1 < self.nz))
        def _():
            self.up(zz).start()

        @pl.when((zz > self.z) & (self.z > 0))
        def _():
            self.down(zz).start()

        self.across(zz, 0).start()

    def spread(self, zz):
        self.to_x(zz).start()
        self.to_y(zz).start()

    def plane(self, zz):
        self.wait_recv(zz, 1)
        self.on_y(zz).start()
        self.across(zz, 1).start()
        self.wait_recv(zz, 2)
        self.on_x(zz).start()
        self.across(zz, 2).start()

    def diagonal(self, zz):
        for kind in (3, 4):
            self.wait_recv(zz, kind)
            self.across(zz, kind).start()

    def both(self, s, what):
        @pl.when((s >= 1) & (self.z - s >= 0))
        def _():
            what(self.z - s)

        @pl.when((s >= 1) & (self.z + s < self.nz))
        def _():
            what(self.z + s)

    def step(self, s):
        self.both(s - 1, self.plane)
        self.both(s - 2, self.diagonal)

    def finish(self):
        def settle(zz, carry):
            @pl.when(zz != self.z)
            def _():
                for kind in range(len(self.ranges)):
                    self.copy(
                        zz, 1 - self.c, self.ranges[kind], 5 + kind, 5 + kind, self.sibling
                    ).wait_recv()

            @pl.when(zz == self.z)
            def _():
                self.copy(zz, 1 - self.c, self.whole, 5, 5, self.sibling).wait_recv()

            return carry

        lax.fori_loop(0, self.nz, settle, 0)

    def sent(self):
        def settle(zz, carry):
            @pl.when(zz != self.z)
            def _():
                @pl.when((zz < self.z) & (self.z + 1 < self.nz))
                def _():
                    self.up(zz).wait_send()

                @pl.when((zz > self.z) & (self.z > 0))
                def _():
                    self.down(zz).wait_send()

                if self.split:
                    self.to_x(zz).wait_send()
                    self.to_y(zz).wait_send()
                    self.on_y(zz).wait_send()
                    self.on_x(zz).wait_send()
                for kind in range(len(self.ranges)):
                    self.across(zz, kind).wait_send()

            return carry

        lax.fori_loop(0, self.nz, settle, 0)

        @pl.when(self.z + 1 < self.nz)
        def _():
            self.up(self.z, True).wait_send()

        @pl.when(self.z > 0)
        def _():
            self.down(self.z, True).wait_send()

        self.across_own().wait_send()


def kernel(
    nt, ng,
    owner_ref, freq_ref, hidden_ref, ids_ref, prefix_ref, ngain_ref, qgain_ref, kgain_ref,
    wq_ref, wo_ref,
    out_ref, key_ref, value_ref,
    wq, wo, pall, psel, kv, ids_buf, normed, queries, attended, bias,
    k_send, k_recv,
    q_send, q_recv, o_send, o_recv, p_send, p_recv, pa_send, pa_recv,
    id_send, id_recv, kv_send, kv_recv,
):
    g, t = lax.axis_index("grp"), lax.axis_index("tok")
    nz = nt // 2
    z, c = t // 2, t % 2
    rows = hidden_ref.shape[1]
    head = qgain_ref.shape[1]
    kvw = key_ref.shape[2]
    kv_heads = kvw // head
    qkvw = wq.shape[2]
    qw = qkvw - 2 * kvw
    ratio = (qw // head) // kv_heads
    depth = wq.shape[0] * wq.shape[1]

    barrier = pltpu.get_barrier_semaphore()

    def greet_tok(k, carry):
        pl.semaphore_signal(
            barrier, inc=1, device_id=(g, (t + k) % nt), device_id_type=MESH
        )
        return carry

    lax.fori_loop(1, nt, greet_tok, 0)
    for k in range(1, ng):
        pl.semaphore_signal(
            barrier, inc=1, device_id=((g + k) % ng, t), device_id_type=MESH
        )
    ids = ids_ref[...]
    ids_buf[0] = jnp.broadcast_to(ids, ids_buf.shape[1:])
    for back in range(1, REACH + 1):
        @pl.when(t < back)
        def _():
            ids_buf[back] = jnp.full(ids_buf.shape[1:], -1, jnp.int32)
            kv[back] = jnp.zeros(kv.shape[1:], kv.dtype)
    pl.semaphore_wait(barrier, nt - 1 + ng - 1)

    kg = Gather(wq_ref, wq, k_send, k_recv, nz, True, qw, 2 * kvw)
    qg = Gather(wq_ref, wq, q_send, q_recv, nz, True, 0, qw)
    og = Gather(wo_ref, wo, o_send, o_recv, nz, True)
    pg = Gather(psel.at[t], psel, p_send, p_recv, nz, False)

    def id_copy(back):
        return pltpu.make_async_remote_copy(
            src_ref=ids_buf.at[0], dst_ref=ids_buf.at[back],
            send_sem=id_send.at[back], recv_sem=id_recv.at[back],
            device_id=(g, (t + back) % nt), device_id_type=MESH,
        )

    for back in range(1, REACH + 1):
        @pl.when(t + back < nt)
        def _():
            id_copy(back).start()

    def prefix_copy(k):
        return pltpu.make_async_remote_copy(
            src_ref=prefix_ref.at[0], dst_ref=pall.at[g],
            send_sem=pa_send.at[k], recv_sem=pa_recv.at[k],
            device_id=((g + k) % ng, t), device_id_type=MESH,
        )

    def prefix_got(k):
        return pltpu.make_async_remote_copy(
            src_ref=prefix_ref.at[0], dst_ref=pall.at[(g + ng - k) % ng],
            send_sem=pa_send.at[k], recv_sem=pa_recv.at[k],
            device_id=((g + k) % ng, t), device_id_type=MESH,
        )

    for k in range(1, ng):
        prefix_copy(k).start()
    kg.start()

    wq[t] = wq_ref[...]
    wo[t] = wo_ref[...]
    pall[g] = prefix_ref[0]

    def norm_rows(i, carry):
        at = pl.ds(pl.multiple_of(i * 64, 64), 64)
        x = hidden_ref[0, at, :].astype(jnp.float32)
        x = x * lax.rsqrt(jnp.mean(x * x, axis=-1, keepdims=True) + epsilon)
        normed[at, :] = (x * ngain_ref[...].astype(jnp.float32).reshape(1, -1)).astype(jnp.bfloat16)
        return carry

    lax.fori_loop(0, rows // 64, norm_rows, 0)

    for k in range(1, ng):
        prefix_got(k).wait_recv()
    psel[t] = pall[owner_ref[g]]

    for back in range(1, REACH + 1):
        @pl.when(t >= back)
        def _():
            id_copy(back).wait_recv()
    column = jnp.transpose(
        jnp.broadcast_to(ids.astype(jnp.float32), (128, rows)), (1, 0)
    )[:, :1]
    here = lax.broadcasted_iota(jnp.int32, (rows, rows), 0)
    there = lax.broadcasted_iota(jnp.int32, (rows, rows), 1)
    count = jnp.zeros((rows, 1), jnp.float32)
    for back in range(REACH + 1):
        allowed = column == ids_buf[back, 0:1, :].astype(jnp.float32)
        if back == 0:
            allowed = allowed & (there <= here)
        count += jnp.sum(jnp.where(allowed, 1.0, 0.0), axis=-1, keepdims=True)
        bias[back] = jnp.where(allowed, 0.0, floor_score)
    prefix_len = psel.shape[0] * psel.shape[1]
    position = count + (prefix_len - 1.0)
    angles = position * freq_ref[...]
    cosine = jnp.cos(angles)
    lane = lax.broadcasted_iota(jnp.int32, (rows, head), 1)
    sine = jnp.sin(angles)
    sine = jnp.where(lane < head // 2, -sine, sine)

    def first(s, carry):
        kg.both(s, kg.arrive)
        kg.both(s, kg.spread)
        kg.step(s)
        return carry

    lax.fori_loop(1, nz, first, 0)
    qg.start()
    pg.start()

    def second(s, carry):
        qg.both(s, qg.arrive)
        kg.step(nz - 1 + s)
        qg.both(s, qg.spread)
        return carry

    lax.fori_loop(1, nz, second, 0)
    og.start()
    kg.finish()

    def project(j):
        at = pl.ds(pl.multiple_of(j * BLOCK, BLOCK), BLOCK)
        w = wq[:, :, at].reshape(depth, BLOCK)
        return jnp.dot(normed[...], w, preferred_element_type=jnp.float32)

    def turned(block, gain):
        parts = []
        for i in range(BLOCK // head):
            a = block[:, i * head:(i + 1) * head]
            a = a * lax.rsqrt(jnp.mean(a * a, axis=-1, keepdims=True) + epsilon)
            a = a * gain
            a = a * cosine + pltpu.roll(a, head // 2, 1) * sine
            parts.append(a.astype(jnp.bfloat16))
        return jnp.concatenate(parts, axis=1)

    def key_block(j, carry):
        at = pl.ds(pl.multiple_of(j * BLOCK, BLOCK), BLOCK)
        made = turned(project(qw // BLOCK + j), kgain_ref[...].astype(jnp.float32))
        kv[0, :, at] = made
        key_ref[0, :, at] = made
        return carry

    def value_block(j, carry):
        made = project((qw + kvw) // BLOCK + j).astype(jnp.bfloat16)
        kv[0, :, pl.ds(pl.multiple_of(kvw + j * BLOCK, BLOCK), BLOCK)] = made
        value_ref[0, :, pl.ds(pl.multiple_of(j * BLOCK, BLOCK), BLOCK)] = made
        return carry

    def query_block(j, carry):
        at = pl.ds(pl.multiple_of(j * BLOCK, BLOCK), BLOCK)
        queries[:, at] = turned(project(j), qgain_ref[...].astype(jnp.float32))
        return carry

    def out_arrive(s, carry):
        og.both(s, og.arrive)
        return carry

    lax.fori_loop(0, kvw // BLOCK, key_block, 0)
    out_arrive(1, 0)
    lax.fori_loop(0, kvw // BLOCK, value_block, 0)

    def kv_copy(src, dst, dev):
        return pltpu.make_async_remote_copy(
            src_ref=kv.at[src], dst_ref=kv.at[dst],
            send_sem=kv_send.at[dst], recv_sem=kv_recv.at[dst],
            device_id=(g, dev), device_id_type=MESH,
        )

    to_next = kv_copy(0, 2, (t + 2) % nt)
    beside = kv_copy(0, 1, z * 2 + 1 - c)
    passed_on = kv_copy(2, 1, z * 2 + 1 - c)

    @pl.when(t + 2 < nt)
    def _():
        to_next.start()

    @pl.when(c == 0)
    def _():
        beside.start()

    def third(s, carry):
        pg.both(s, pg.arrive)
        qg.step(s + 1)
        return carry

    lax.fori_loop(1, nz, third, 0)
    lax.fori_loop(2, nz, out_arrive, 0)

    def out_spread(s, carry):
        og.both(s, og.spread)
        return carry

    lax.fori_loop(1, nz, out_spread, 0)
    qg.step(nz + 1)
    qg.finish()
    lax.fori_loop(0, qw // BLOCK, query_block, 0)
    pg.finish()

    def fourth(s, carry):
        og.step(s)
        return carry


    for one in (kg, qg, pg):
        one.sent()
    for k in range(1, ng):
        prefix_copy(k).wait_send()
    for back in range(1, REACH + 1):
        @pl.when(t + back < nt)
        def _():
            id_copy(back).wait_send()

    @pl.when(t >= 2)
    def _():
        to_next.wait_recv()

    @pl.when((c == 1) & (z > 0))
    def _():
        passed_on.start()

    @pl.when(t >= 1)
    def _():
        beside.wait_recv()

    factor = head ** (-0.5) * math.log2(math.e)
    dims = (((1,), (1,)), ((), ()))

    def attend(h, carry):
        kat = pl.ds(pl.multiple_of(h * head, head), head)
        vat = pl.ds(pl.multiple_of(kvw + h * head, head), head)
        q = jnp.concatenate(
            [
                queries[:, pl.ds(pl.multiple_of((h * ratio + r) * head, head), head)]
                for r in range(ratio)
            ],
            axis=0,
        )
        keys = [psel[:, :, kat].reshape(prefix_len, head)]
        values = [psel[:, :, vat].reshape(prefix_len, head)]
        for back in range(REACH + 1):
            keys.append(kv[back, :, kat])
            values.append(kv[back, :, vat])
        scores = []
        for i, k in enumerate(keys):
            s = lax.dot_general(q, k, dims, preferred_element_type=jnp.float32)
            if i:
                s = (s.reshape(ratio, rows, rows) + bias[i - 1][None]).reshape(ratio * rows, rows)
            scores.append(s)
        top = functools.reduce(
            jnp.maximum, [jnp.max(s, axis=-1, keepdims=True) for s in scores]
        )
        total, mixed = 0.0, 0.0
        for s, v in zip(scores, values):
            p = jnp.exp2((s - top) * factor)
            total += jnp.sum(p, axis=-1, keepdims=True)
            mixed += jnp.dot(p.astype(jnp.bfloat16), v, preferred_element_type=jnp.float32)
        mixed = (mixed / total).astype(jnp.bfloat16)
        for r in range(ratio):
            attended[:, pl.ds(pl.multiple_of((h * ratio + r) * head, head), head)] = mixed[
                r * rows:(r + 1) * rows
            ]

        lax.fori_loop(2 + h * per, jnp.minimum(2 + (h + 1) * per, nz + 2), fourth, 0)
        return carry

    per = -(-nz // kv_heads)
    lax.fori_loop(0, kv_heads, attend, 0)
    og.finish()

    def out_block(j, carry):
        at = pl.ds(pl.multiple_of(j * BLOCK, BLOCK), BLOCK)
        w = wo[:, :, at].reshape(qw, BLOCK)
        out_ref[0, :, at] = jnp.dot(
            attended[...], w, preferred_element_type=jnp.float32
        ).astype(jnp.bfloat16)
        return carry

    lax.fori_loop(0, out_ref.shape[2] // BLOCK, out_block, 0)

    og.sent()

    @pl.when(t + 2 < nt)
    def _():
        to_next.wait_send()

    @pl.when(c == 0)
    def _():
        beside.wait_send()

    @pl.when((c == 1) & (z > 0))
    def _():
        passed_on.wait_send()


def place(*refs):
    count = (len(refs) - 1) // 2
    sems = refs[-1]
    copies = []
    for i in range(count):
        rows = refs[i].shape[1] // 4
        for j in range(4):
            at = pl.ds(j * rows, rows)
            copies.append(
                pltpu.make_async_copy(
                    refs[i].at[:, at], refs[count + i].at[:, at], sems.at[i, j]
                )
            )
    for one in copies:
        one.start()
    for one in copies:
        one.wait()


def per_device(
    nt, ng,
    hidden_in, doc_ids, prefix_kv, prefix_owner, norm_gain, query_gain, key_norm_gain, w_qkv, w_out
):
    rows, width = hidden_in.shape[1:]
    head = query_gain.shape[0]
    kvw = prefix_kv.shape[2] // 2
    pre = prefix_kv.shape[1]
    qkvw = w_qkv.shape[1]
    qw = qkvw - 2 * kvw
    nz = nt // 2
    half = head // 2
    freqs = np.float32(theta_base) ** (-np.arange(half, dtype=np.float32) / np.float32(half))
    freqs = np.concatenate([freqs, freqs]).astype(np.float32)[None]
    bf = jnp.bfloat16
    vm = pl.BlockSpec(memory_space=pltpu.VMEM)
    dma = pltpu.SemaphoreType.DMA
    made = pl.pallas_call(
        functools.partial(kernel, nt, ng),
        out_shape=(
            pltpu.VMEM((1, rows, w_out.shape[1]), bf),
            pltpu.VMEM((1, rows, kvw), bf),
            pltpu.VMEM((1, rows, kvw), bf),
        ),
        in_specs=[pl.BlockSpec(memory_space=pltpu.SMEM)] + [vm] * 9,
        out_specs=(vm, vm, vm),
        scratch_shapes=[
            pltpu.VMEM((nt,) + w_qkv.shape, bf),
            pltpu.VMEM((nt,) + w_out.shape, bf),
            pltpu.VMEM((ng, pre, 2 * kvw), bf),
            pltpu.VMEM((nt, pre, 2 * kvw), bf),
            pltpu.VMEM((REACH + 1, rows, 2 * kvw), bf),
            pltpu.VMEM((REACH + 1, 8, rows), jnp.int32),
            pltpu.VMEM((rows, width), bf),
            pltpu.VMEM((rows, qw), bf),
            pltpu.VMEM((rows, qw), bf),
            pltpu.VMEM((REACH + 1, rows, rows), jnp.float32),
            dma((10, nz)), dma((10, nz)),
            dma((10, nz)), dma((10, nz)),
            dma((10, nz)), dma((10, nz)),
            dma((10, nz)), dma((10, nz)),
            dma((ng,)), dma((ng,)),
            dma((REACH + 1,)), dma((REACH + 1,)),
            dma((REACH + 1,)), dma((REACH + 1,)),
        ],
        compiler_params=pltpu.CompilerParams(
            collective_id=0, has_side_effects=True, vmem_limit_bytes=56 * 1024 * 1024
        ),
    )(
        prefix_owner, jnp.asarray(freqs), hidden_in, doc_ids, prefix_kv,
        norm_gain, query_gain[None], key_norm_gain[None], w_qkv, w_out,
    )
    return pl.pallas_call(
        place,
        out_shape=tuple(jax.ShapeDtypeStruct(x.shape, x.dtype) for x in made),
        in_specs=[vm] * len(made),
        out_specs=(pl.BlockSpec(memory_space=pl.ANY),) * len(made),
        scratch_shapes=[dma((len(made), 4))],
        compiler_params=pltpu.CompilerParams(vmem_limit_bytes=1024 * 1024),
    )(*made)


def solution(mesh):
    return jax.shard_map(
        functools.partial(per_device, mesh.shape["tok"], mesh.shape["grp"]),
        mesh=mesh,
        in_specs=(
            P("grp", "tok", None),
            P("grp", "tok"),
            P("grp", "tok", None),
            P(),
            P(),
            P(),
            P(),
            P("tok", None),
            P("tok", None),
        ),
        out_specs=(P("grp", "tok", None), P("grp", "tok", None), P("grp", "tok", None)),
        check_vma=False,
    )
```

```python
import functools
import math

import jax
import jax.numpy as jnp
import numpy as np
from jax import lax
from jax.experimental import pallas as pl
from jax.experimental.pallas import tpu as pltpu
from jax.sharding import PartitionSpec as P

MESH = pl.DeviceIdType.MESH
epsilon = 1e-06
theta_base = 1000000.0
floor_score = -1e30
REACH = 2
BLOCK = 256


class Gather:
    def __init__(self, own, buf, send, recv, nz, split, base=0, width=None):
        self.own, self.buf, self.send, self.recv = own, buf, send, recv
        self.nz, self.split = nz, split
        g, t = lax.axis_index("grp"), lax.axis_index("tok")
        self.g, self.t = g, t
        self.z, self.c = t // 2, t % 2
        self.gx = g + 1 - 2 * (g % 2)
        self.gy = (g + 2) % 4
        self.gd = (self.gx + 2) % 4
        width = buf.shape[2] if width is None else width
        rows = buf.shape[1]
        self.whole = (0, rows, base, width)
        if not split:
            self.ranges = (self.whole,)
            return
        q = width // 4
        parts = [(0, rows, base + i * q, q) for i in (self.g, self.gx, self.gy, self.gd)]
        self.ranges = tuple(parts[:3]) + tuple(self.half(parts[3], i) for i in range(2))

    def half(self, part, i):
        row, rows, col, cols = part
        return (row, rows, col + i * (cols // 2), cols // 2)

    def at(self, ref, row, rows, col, cols):
        row = row if isinstance(row, int) else pl.multiple_of(row, 16)
        col = col if isinstance(col, int) else pl.multiple_of(col, 128)
        return ref.at[pl.ds(row, rows), pl.ds(col, cols)]

    def copy(self, zz, core, part, s, r, dev, own=False):
        place = self.at(self.buf.at[zz * 2 + core], *part)
        src = self.at(self.own, *part) if own else place
        return pltpu.make_async_remote_copy(
            src_ref=src,
            dst_ref=place,
            send_sem=self.send.at[s, zz],
            recv_sem=self.recv.at[r, zz],
            device_id=dev,
            device_id_type=MESH,
        )

    def dev_z(self, zz):
        return (self.g, zz * 2 + self.c)

    @property
    def sibling(self):
        return (self.g, self.z * 2 + 1 - self.c)

    def up(self, zz, own=False):
        return self.copy(zz, self.c, self.ranges[0], 0, 0, self.dev_z(self.z + 1), own)

    def down(self, zz, own=False):
        return self.copy(zz, self.c, self.ranges[0], 1 if own else 0, 0, self.dev_z(self.z - 1), own)

    def to_x(self, zz):
        return self.copy(zz, self.c, self.ranges[0], 1, 1, (self.gx, self.t))

    def to_y(self, zz):
        return self.copy(zz, self.c, self.ranges[0], 2, 2, (self.gy, self.t))

    def on_y(self, zz):
        return self.copy(zz, self.c, self.half(self.ranges[1], 0), 3, 3, (self.gy, self.t))

    def on_x(self, zz):
        return self.copy(zz, self.c, self.half(self.ranges[2], 1), 4, 4, (self.gx, self.t))

    def across(self, zz, kind):
        return self.copy(zz, self.c, self.ranges[kind], 5 + kind, 5 + kind, self.sibling)

    def across_own(self):
        return self.copy(self.z, self.c, self.whole, 5, 5, self.sibling, True)

    def wait_recv(self, zz, kind):
        self.copy(zz, self.c, self.ranges[kind], kind, kind, self.sibling).wait_recv()

    def start(self):
        @pl.when(self.z + 1 < self.nz)
        def _():
            self.up(self.z, True).start()

        @pl.when(self.z > 0)
        def _():
            self.down(self.z, True).start()

        self.across_own().start()

    def arrive(self, zz):
        self.wait_recv(zz, 0)

        @pl.when((zz < self.z) & (self.z + 1 < self.nz))
        def _():
            self.up(zz).start()

        @pl.when((zz > self.z) & (self.z > 0))
        def _():
            self.down(zz).start()

        self.across(zz, 0).start()

    def spread(self, zz):
        self.to_x(zz).start()
        self.to_y(zz).start()

    def plane(self, zz):
        self.wait_recv(zz, 1)
        self.on_y(zz).start()
        self.across(zz, 1).start()
        self.wait_recv(zz, 2)
        self.on_x(zz).start()
        self.across(zz, 2).start()

    def diagonal(self, zz):
        for kind in (3, 4):
            self.wait_recv(zz, kind)
            self.across(zz, kind).start()

    def both(self, s, what):
        @pl.when((s >= 1) & (self.z - s >= 0))
        def _():
            what(self.z - s)

        @pl.when((s >= 1) & (self.z + s < self.nz))
        def _():
            what(self.z + s)

    def step(self, s):
        self.both(s - 1, self.plane)
        self.both(s - 2, self.diagonal)

    def finish(self):
        def settle(zz, carry):
            @pl.when(zz != self.z)
            def _():
                for kind in range(len(self.ranges)):
                    self.copy(
                        zz, 1 - self.c, self.ranges[kind], 5 + kind, 5 + kind, self.sibling
                    ).wait_recv()

            @pl.when(zz == self.z)
            def _():
                self.copy(zz, 1 - self.c, self.whole, 5, 5, self.sibling).wait_recv()

            return carry

        lax.fori_loop(0, self.nz, settle, 0)

    def sent(self):
        def settle(zz, carry):
            @pl.when(zz != self.z)
            def _():
                @pl.when((zz < self.z) & (self.z + 1 < self.nz))
                def _():
                    self.up(zz).wait_send()

                @pl.when((zz > self.z) & (self.z > 0))
                def _():
                    self.down(zz).wait_send()

                if self.split:
                    self.to_x(zz).wait_send()
                    self.to_y(zz).wait_send()
                    self.on_y(zz).wait_send()
                    self.on_x(zz).wait_send()
                for kind in range(len(self.ranges)):
                    self.across(zz, kind).wait_send()

            return carry

        lax.fori_loop(0, self.nz, settle, 0)

        @pl.when(self.z + 1 < self.nz)
        def _():
            self.up(self.z, True).wait_send()

        @pl.when(self.z > 0)
        def _():
            self.down(self.z, True).wait_send()

        self.across_own().wait_send()


def kernel(
    nt, ng,
    owner_ref, freq_ref, hidden_ref, ids_ref, prefix_ref, ngain_ref, qgain_ref, kgain_ref,
    wq_ref, wo_ref,
    out_ref, key_ref, value_ref,
    wq, wo, pall, psel, kv, ids_buf, normed, queries, attended, bias,
    k_send, k_recv,
    q_send, q_recv, o_send, o_recv, p_send, p_recv, pa_send, pa_recv,
    id_send, id_recv, kv_send, kv_recv,
):
    g, t = lax.axis_index("grp"), lax.axis_index("tok")
    nz = nt // 2
    z, c = t // 2, t % 2
    rows = hidden_ref.shape[1]
    head = qgain_ref.shape[1]
    kvw = key_ref.shape[2]
    kv_heads = kvw // head
    qkvw = wq.shape[2]
    qw = qkvw - 2 * kvw
    ratio = (qw // head) // kv_heads
    depth = wq.shape[0] * wq.shape[1]

    barrier = pltpu.get_barrier_semaphore()

    def greet_tok(k, carry):
        pl.semaphore_signal(
            barrier, inc=1, device_id=(g, (t + k) % nt), device_id_type=MESH
        )
        return carry

    lax.fori_loop(1, nt, greet_tok, 0)
    for k in range(1, ng):
        pl.semaphore_signal(
            barrier, inc=1, device_id=((g + k) % ng, t), device_id_type=MESH
        )
    ids = ids_ref[...]
    ids_buf[0] = jnp.broadcast_to(ids, ids_buf.shape[1:])
    for back in range(1, REACH + 1):
        @pl.when(t < back)
        def _():
            ids_buf[back] = jnp.full(ids_buf.shape[1:], -1, jnp.int32)
            kv[back] = jnp.zeros(kv.shape[1:], kv.dtype)
    pl.semaphore_wait(barrier, nt - 1 + ng - 1)

    kg = Gather(wq_ref, wq, k_send, k_recv, nz, True, qw, 2 * kvw)
    qg = Gather(wq_ref, wq, q_send, q_recv, nz, True, 0, qw)
    og = Gather(wo_ref, wo, o_send, o_recv, nz, True)
    pg = Gather(psel.at[t], psel, p_send, p_recv, nz, False)

    def id_copy(back):
        return pltpu.make_async_remote_copy(
            src_ref=ids_buf.at[0], dst_ref=ids_buf.at[back],
            send_sem=id_send.at[back], recv_sem=id_recv.at[back],
            device_id=(g, (t + back) % nt), device_id_type=MESH,
        )

    for back in range(1, REACH + 1):
        @pl.when(t + back < nt)
        def _():
            id_copy(back).start()

    def prefix_copy(k):
        return pltpu.make_async_remote_copy(
            src_ref=prefix_ref.at[0], dst_ref=pall.at[g],
            send_sem=pa_send.at[k], recv_sem=pa_recv.at[k],
            device_id=((g + k) % ng, t), device_id_type=MESH,
        )

    def prefix_got(k):
        return pltpu.make_async_remote_copy(
            src_ref=prefix_ref.at[0], dst_ref=pall.at[(g + ng - k) % ng],
            send_sem=pa_send.at[k], recv_sem=pa_recv.at[k],
            device_id=((g + k) % ng, t), device_id_type=MESH,
        )

    for k in range(1, ng):
        prefix_copy(k).start()
    kg.start()

    wq[t] = wq_ref[...]
    wo[t] = wo_ref[...]
    pall[g] = prefix_ref[0]

    def norm_rows(i, carry):
        at = pl.ds(pl.multiple_of(i * 64, 64), 64)
        x = hidden_ref[0, at, :].astype(jnp.float32)
        x = x * lax.rsqrt(jnp.mean(x * x, axis=-1, keepdims=True) + epsilon)
        normed[at, :] = (x * ngain_ref[...].astype(jnp.float32).reshape(1, -1)).astype(jnp.bfloat16)
        return carry

    lax.fori_loop(0, rows // 64, norm_rows, 0)

    for k in range(1, ng):
        prefix_got(k).wait_recv()
    psel[t] = pall[owner_ref[g]]

    for back in range(1, REACH + 1):
        @pl.when(t >= back)
        def _():
            id_copy(back).wait_recv()
    column = jnp.transpose(
        jnp.broadcast_to(ids.astype(jnp.float32), (128, rows)), (1, 0)
    )[:, :1]
    here = lax.broadcasted_iota(jnp.int32, (rows, rows), 0)
    there = lax.broadcasted_iota(jnp.int32, (rows, rows), 1)
    count = jnp.zeros((rows, 1), jnp.float32)
    for back in range(REACH + 1):
        allowed = column == ids_buf[back, 0:1, :].astype(jnp.float32)
        if back == 0:
            allowed = allowed & (there <= here)
        count += jnp.sum(jnp.where(allowed, 1.0, 0.0), axis=-1, keepdims=True)
        bias[back] = jnp.where(allowed, 0.0, floor_score)
    prefix_len = psel.shape[0] * psel.shape[1]
    position = count + (prefix_len - 1.0)
    angles = position * freq_ref[...]
    cosine = jnp.cos(angles)
    lane = lax.broadcasted_iota(jnp.int32, (rows, head), 1)
    sine = jnp.sin(angles)
    sine = jnp.where(lane < head // 2, -sine, sine)

    def first(s, carry):
        kg.both(s, kg.arrive)
        kg.both(s, kg.spread)
        kg.step(s)
        return carry

    lax.fori_loop(1, nz, first, 0)
    qg.start()
    pg.start()

    def second(s, carry):
        qg.both(s, qg.arrive)
        kg.step(nz - 1 + s)
        qg.both(s, qg.spread)
        return carry

    lax.fori_loop(1, nz, second, 0)
    og.start()
    kg.finish()

    def project(j):
        at = pl.ds(pl.multiple_of(j * BLOCK, BLOCK), BLOCK)
        w = wq[:, :, at].reshape(depth, BLOCK)
        return jnp.dot(normed[...], w, preferred_element_type=jnp.float32)

    def turned(block, gain):
        parts = []
        for i in range(BLOCK // head):
            a = block[:, i * head:(i + 1) * head]
            a = a * lax.rsqrt(jnp.mean(a * a, axis=-1, keepdims=True) + epsilon)
            a = a * gain
            a = a * cosine + pltpu.roll(a, head // 2, 1) * sine
            parts.append(a.astype(jnp.bfloat16))
        return jnp.concatenate(parts, axis=1)

    def key_block(j, carry):
        at = pl.ds(pl.multiple_of(j * BLOCK, BLOCK), BLOCK)
        made = turned(project(qw // BLOCK + j), kgain_ref[...].astype(jnp.float32))
        kv[0, :, at] = made
        key_ref[0, :, at] = made
        return carry

    def value_block(j, carry):
        made = project((qw + kvw) // BLOCK + j).astype(jnp.bfloat16)
        kv[0, :, pl.ds(pl.multiple_of(kvw + j * BLOCK, BLOCK), BLOCK)] = made
        value_ref[0, :, pl.ds(pl.multiple_of(j * BLOCK, BLOCK), BLOCK)] = made
        return carry

    def query_block(j, carry):
        at = pl.ds(pl.multiple_of(j * BLOCK, BLOCK), BLOCK)
        queries[:, at] = turned(project(j), qgain_ref[...].astype(jnp.float32))
        return carry

    def out_arrive(s, carry):
        og.both(s, og.arrive)
        return carry

    lax.fori_loop(0, kvw // BLOCK, key_block, 0)
    out_arrive(1, 0)
    lax.fori_loop(0, kvw // BLOCK, value_block, 0)

    def kv_copy(src, dst, dev):
        return pltpu.make_async_remote_copy(
            src_ref=kv.at[src], dst_ref=kv.at[dst],
            send_sem=kv_send.at[dst], recv_sem=kv_recv.at[dst],
            device_id=(g, dev), device_id_type=MESH,
        )

    to_next = kv_copy(0, 2, (t + 2) % nt)
    beside = kv_copy(0, 1, z * 2 + 1 - c)
    passed_on = kv_copy(2, 1, z * 2 + 1 - c)

    @pl.when(t + 2 < nt)
    def _():
        to_next.start()

    @pl.when(c == 0)
    def _():
        beside.start()

    def third(s, carry):
        pg.both(s, pg.arrive)
        qg.step(s + 1)

        @pl.when(s >= 2)
        def _():
            og.both(s, og.arrive)

        og.both(s, og.spread)
        return carry

    lax.fori_loop(1, nz, third, 0)
    qg.step(nz + 1)
    qg.finish()
    lax.fori_loop(0, qw // BLOCK, query_block, 0)
    pg.finish()

    def fourth(s, carry):
        og.step(s)
        return carry


    for one in (kg, qg, pg):
        one.sent()
    for k in range(1, ng):
        prefix_copy(k).wait_send()
    for back in range(1, REACH + 1):
        @pl.when(t + back < nt)
        def _():
            id_copy(back).wait_send()

    @pl.when(t >= 2)
    def _():
        to_next.wait_recv()

    @pl.when((c == 1) & (z > 0))
    def _():
        passed_on.start()

    @pl.when(t >= 1)
    def _():
        beside.wait_recv()

    factor = head ** (-0.5) * math.log2(math.e)
    dims = (((1,), (1,)), ((), ()))

    def attend(h, carry):
        kat = pl.ds(pl.multiple_of(h * head, head), head)
        vat = pl.ds(pl.multiple_of(kvw + h * head, head), head)
        q = jnp.concatenate(
            [
                queries[:, pl.ds(pl.multiple_of((h * ratio + r) * head, head), head)]
                for r in range(ratio)
            ],
            axis=0,
        )
        keys = [psel[:, :, kat].reshape(prefix_len, head)]
        values = [psel[:, :, vat].reshape(prefix_len, head)]
        for back in range(REACH + 1):
            keys.append(kv[back, :, kat])
            values.append(kv[back, :, vat])
        scores = []
        for i, k in enumerate(keys):
            s = lax.dot_general(q, k, dims, preferred_element_type=jnp.float32)
            if i:
                s = (s.reshape(ratio, rows, rows) + bias[i - 1][None]).reshape(ratio * rows, rows)
            scores.append(s)
        top = functools.reduce(
            jnp.maximum, [jnp.max(s, axis=-1, keepdims=True) for s in scores]
        )
        total, mixed = 0.0, 0.0
        for s, v in zip(scores, values):
            p = jnp.exp2((s - top) * factor)
            total += jnp.sum(p, axis=-1, keepdims=True)
            mixed += jnp.dot(p.astype(jnp.bfloat16), v, preferred_element_type=jnp.float32)
        mixed = (mixed / total).astype(jnp.bfloat16)
        for r in range(ratio):
            attended[:, pl.ds(pl.multiple_of((h * ratio + r) * head, head), head)] = mixed[
                r * rows:(r + 1) * rows
            ]

        lax.fori_loop(2 + h * per, jnp.minimum(2 + (h + 1) * per, nz + 2), fourth, 0)
        return carry

    per = -(-nz // kv_heads)
    lax.fori_loop(0, kv_heads, attend, 0)
    og.finish()

    def out_block(j, carry):
        at = pl.ds(pl.multiple_of(j * BLOCK, BLOCK), BLOCK)
        w = wo[:, :, at].reshape(qw, BLOCK)
        out_ref[0, :, at] = jnp.dot(
            attended[...], w, preferred_element_type=jnp.float32
        ).astype(jnp.bfloat16)
        return carry

    lax.fori_loop(0, out_ref.shape[2] // BLOCK, out_block, 0)

    og.sent()

    @pl.when(t + 2 < nt)
    def _():
        to_next.wait_send()

    @pl.when(c == 0)
    def _():
        beside.wait_send()

    @pl.when((c == 1) & (z > 0))
    def _():
        passed_on.wait_send()


def place(*refs):
    count = (len(refs) - 1) // 2
    sems = refs[-1]
    copies = []
    for i in range(count):
        rows = refs[i].shape[1] // 4
        for j in range(4):
            at = pl.ds(j * rows, rows)
            copies.append(
                pltpu.make_async_copy(
                    refs[i].at[:, at], refs[count + i].at[:, at], sems.at[i, j]
                )
            )
    for one in copies:
        one.start()
    for one in copies:
        one.wait()


def per_device(
    nt, ng,
    hidden_in, doc_ids, prefix_kv, prefix_owner, norm_gain, query_gain, key_norm_gain, w_qkv, w_out
):
    rows, width = hidden_in.shape[1:]
    head = query_gain.shape[0]
    kvw = prefix_kv.shape[2] // 2
    pre = prefix_kv.shape[1]
    qkvw = w_qkv.shape[1]
    qw = qkvw - 2 * kvw
    nz = nt // 2
    half = head // 2
    freqs = np.float32(theta_base) ** (-np.arange(half, dtype=np.float32) / np.float32(half))
    freqs = np.concatenate([freqs, freqs]).astype(np.float32)[None]
    bf = jnp.bfloat16
    vm = pl.BlockSpec(memory_space=pltpu.VMEM)
    dma = pltpu.SemaphoreType.DMA
    made = pl.pallas_call(
        functools.partial(kernel, nt, ng),
        out_shape=(
            pltpu.VMEM((1, rows, w_out.shape[1]), bf),
            pltpu.VMEM((1, rows, kvw), bf),
            pltpu.VMEM((1, rows, kvw), bf),
        ),
        in_specs=[pl.BlockSpec(memory_space=pltpu.SMEM)] + [vm] * 9,
        out_specs=(vm, vm, vm),
        scratch_shapes=[
            pltpu.VMEM((nt,) + w_qkv.shape, bf),
            pltpu.VMEM((nt,) + w_out.shape, bf),
            pltpu.VMEM((ng, pre, 2 * kvw), bf),
            pltpu.VMEM((nt, pre, 2 * kvw), bf),
            pltpu.VMEM((REACH + 1, rows, 2 * kvw), bf),
            pltpu.VMEM((REACH + 1, 8, rows), jnp.int32),
            pltpu.VMEM((rows, width), bf),
            pltpu.VMEM((rows, qw), bf),
            pltpu.VMEM((rows, qw), bf),
            pltpu.VMEM((REACH + 1, rows, rows), jnp.float32),
            dma((10, nz)), dma((10, nz)),
            dma((10, nz)), dma((10, nz)),
            dma((10, nz)), dma((10, nz)),
            dma((10, nz)), dma((10, nz)),
            dma((ng,)), dma((ng,)),
            dma((REACH + 1,)), dma((REACH + 1,)),
            dma((REACH + 1,)), dma((REACH + 1,)),
        ],
        compiler_params=pltpu.CompilerParams(
            collective_id=0, has_side_effects=True, vmem_limit_bytes=56 * 1024 * 1024
        ),
    )(
        prefix_owner, jnp.asarray(freqs), hidden_in, doc_ids, prefix_kv,
        norm_gain, query_gain[None], key_norm_gain[None], w_qkv, w_out,
    )
    return pl.pallas_call(
        place,
        out_shape=tuple(jax.ShapeDtypeStruct(x.shape, x.dtype) for x in made),
        in_specs=[vm] * len(made),
        out_specs=(pl.BlockSpec(memory_space=pl.ANY),) * len(made),
        scratch_shapes=[dma((len(made), 4))],
        compiler_params=pltpu.CompilerParams(vmem_limit_bytes=1024 * 1024),
    )(*made)


def solution(mesh):
    return jax.shard_map(
        functools.partial(per_device, mesh.shape["tok"], mesh.shape["grp"]),
        mesh=mesh,
        in_specs=(
            P("grp", "tok", None),
            P("grp", "tok"),
            P("grp", "tok", None),
            P(),
            P(),
            P(),
            P(),
            P("tok", None),
            P("tok", None),
        ),
        out_specs=(P("grp", "tok", None), P("grp", "tok", None), P("grp", "tok", None)),
        check_vma=False,
    )
```
